256 devices in a mesh: gx: 16 (over z, core), gy: 16 (over y, x).
Axes of the slice: x: 4, y: 4, z: 8, core: 2. Of those that a mesh axis runs over, the one named last changes fastest.
Arguments:
- velocity: float32 [256, 128, 1024], P('gx', 'gy'), may hold values from -18 to 18
- cotangent: float32 [256, 128, 1024], P('gx', 'gy'), may hold values from -15 to 15
- shape_coef: float32 [256, 1024], P('gx'), may hold values from 0.5 to 4
- patch_map: int32 [256, 1024], P('gx'), may hold values from 0 to 1023
- broken: int32 [1024], P(('gx', 'gy')), may hold values 0 or 1
Outputs:
- new_velocity: float32 [256, 128, 1024], P('gx', 'gy')
- grad_velocity: float32 [256, 128, 1024], P('gx', 'gy')
- patch_sens: float32 [1024], P(('gx', 'gy'))
The draws below stay inside these ranges and needn't reach their ends.
All inputs are finite; a program needn't handle non-finite values. No bound on the sum of `broken` on one device may be relied on, other than what follows from the above.
Results may differ from the reference program's by a relative error of at most 0.0003.
Values sent between devices are 32-bit elements; how exact they have to be, the bound alone decides.
No kernel may reach another device: no remote copies, remote signals or barrier semaphores. Data moves between devices by JAX's collectives and lax.ppermute only.
A program may use at most 64 MiB of HBM per device.

```python
import math
import jax
import jax.numpy as jnp
from jax import lax

X_DEV = 16
NZ = 1024
NX = 256
NY = 128
PATCHES = 1024


def draw_velocity(key, part):
    key = jax.random.fold_in(key, 11)
    key_rough, key_phase = jax.random.split(key, 2)
    phases = jax.random.uniform(key_phase, (2,), jnp.float32, 0.0, 2.0 * math.pi)
    planes = jnp.arange(NX).astype(jnp.float32)[:, None, None]
    cells = jnp.arange(NZ).astype(jnp.float32)[None, None, :]
    along_x = jnp.cos(2.0 * math.pi * planes / NX + phases[0])
    along_z = jnp.cos(2.0 * math.pi * cells / NZ + phases[1])
    rough = 2.5 * jax.random.normal(key_rough, (NX, NY, NZ), jnp.float32)
    return jnp.clip(rough + 9.0 * along_x * along_z, -18.0, 18.0)


def with_ends(array, key, low, top_value):
    extent = array.shape
    index_at = [jax.random.randint(jax.random.fold_in(key, axis), (), 0, extent[axis]) for axis in range(len(extent))]
    array = array.at[tuple(index_at)].set(low)
    longest = extent.index(max(extent))
    index_at[longest] = (index_at[longest] + 1) % extent[longest]
    return array.at[tuple(index_at)].set(top_value)


def block_scale(rng, extent, pieces, least, top_value):
    factor_of, own = 1.0, jax.random.fold_in(rng, 6)
    for dim, parts in pieces:
        steps = jnp.exp(jax.random.uniform(jax.random.fold_in(own, dim), (parts,), jnp.float32, least / len(pieces), top_value / len(pieces)))
        factor_of = factor_of * jnp.repeat(steps, extent[dim] // parts).reshape([-1 if axis == dim else 1 for axis in range(len(extent))])
    return factor_of


def gaussian(own_key, extent, deviation, limit, cuts=(), held_as=jnp.bfloat16):
    gain = block_scale(own_key, extent, cuts, -0.22, 0.18) if cuts else 1.0
    array = jax.random.normal(own_key, extent, jnp.float32) * deviation * gain
    return jnp.minimum(jnp.maximum(array, -limit), limit).astype(held_as)


def setup_inputs(seed: int = 0) -> dict:
    seeds = jax.random.split(jax.random.key(seed), 6)
    return {
        "velocity": draw_velocity(jax.random.fold_in(seeds[5], 71), 0),
        "cotangent": gaussian(seeds[1], (NX, NY, NZ), 3.0, 15.0, ((0, 16), (1, 16)), jnp.float32),
        "shape_coef": jnp.clip(jnp.exp(math.log(4.0) - 2.0794415 * jax.random.uniform(seeds[2], (NX, NZ), jnp.float32) ** block_scale(seeds[2], (NX, NZ), ((0, 16),), -0.2, 0.2)), 0.5, 4.0),
        "patch_map": with_ends(jax.random.randint(seeds[3], (NX, NZ), 0, PATCHES), jax.random.fold_in(seeds[3], 1), 0, PATCHES - 1).astype(jnp.int32),
        "broken": with_ends((jax.random.randint(seeds[4], (PATCHES,), 0, 4) < 1).astype(jnp.int32), jax.random.fold_in(seeds[4], 1), 0, 1),
    }


wall_coef = 0.2
span_coef = 0.15
wall_decay = 8.0

def thomas(diagonal, right_sides, stiffness):

    def down(state_in, row_data):
        upper_prev, reduced_prev = state_in
        diag_row, rhs_row = row_data
        pivot_value = diag_row + stiffness * upper_prev
        upper_now = -stiffness / pivot_value
        reduced_now = (rhs_row + stiffness * reduced_prev) / pivot_value
        return ((upper_now, reduced_now), (upper_now, reduced_now))
    start_state = (jnp.zeros(diagonal.shape[1:], diagonal.dtype), jnp.zeros(right_sides.shape[1:], right_sides.dtype))
    _, (uppers, reduced) = lax.scan(down, start_state, (diagonal, right_sides))

    def upward(next_value, row_data):
        upper_now, reduced_now = row_data
        value_now = reduced_now - upper_now * next_value
        return (value_now, value_now)
    _, solution = lax.scan(upward, jnp.zeros(right_sides.shape[1:], right_sides.dtype), (uppers, reduced), reverse=True)
    return solution

def explicit(field):
    padded = jnp.pad(field, ((0, 0), (1, 1), (0, 0)))
    wall_term = padded[:, 2:, :] + padded[:, :-2, :] - 2.0 * field
    span_term = jnp.roll(field, 1, 2) + jnp.roll(field, -1, 2) - 2.0 * field
    return field + wall_coef * wall_term + span_coef * span_term

def reference(velocity, cotangent, shape_coef, patch_map, broken):
    stiffness = 3.0 * X_DEV * X_DEV
    line_count = NY * NZ
    heights = jnp.arange(NY).astype(velocity.dtype)
    damping = jnp.exp(-wall_decay * heights / NY)
    diagonal = 1.0 + 2.0 * stiffness + shape_coef[:, None, :] * damping[None, :, None]
    forcing = explicit(velocity)
    stacked = jnp.stack([forcing, cotangent], axis=1).reshape(NX, 2, line_count)
    solved = thomas(diagonal.reshape(NX, line_count), stacked, stiffness)
    new_velocity = solved[:, 0].reshape(NX, NY, NZ)
    adjoint = solved[:, 1].reshape(NX, NY, NZ)
    grad_velocity = explicit(adjoint)
    cell_sens = lax.optimization_barrier(jnp.sum(adjoint * new_velocity * damping[None, :, None], axis=1))
    patch_raw = jax.ops.segment_sum(cell_sens.reshape(-1), patch_map.reshape(-1).astype(jnp.int32), num_segments=PATCHES)
    norm_factor = 1.0 / math.sqrt(NX * NY * NZ / PATCHES)
    keep = (1 - broken).astype(velocity.dtype)
    patch_sens = -keep * norm_factor * patch_raw
    return (new_velocity, grad_velocity, patch_sens)
```

```python
import math

import jax
import jax.numpy as jnp
from jax import lax
from jax.experimental import pallas as pl
from jax.experimental.pallas import tpu as pltpu
from jax.sharding import PartitionSpec as P

wall_coef = 0.2
span_coef = 0.15
wall_decay = 8.0
VMEM = pl.BlockSpec(memory_space=pltpu.VMEM)
F32 = jnp.float32
LANES = 128


def shape_of(*dims):
    return jax.ShapeDtypeStruct(dims, F32)


def explicit(field, below, above):
    rows, span = field.shape
    row_ids = lax.broadcasted_iota(jnp.int32, (rows, span), 0)
    lower = jnp.where(row_ids == 0, below, pltpu.roll(field, 1, 0))
    upper = jnp.where(row_ids == rows - 1, above, pltpu.roll(field, rows - 1, 0))
    wall_term = upper + lower - 2.0 * field
    span_term = pltpu.roll(field, 1, 1) + pltpu.roll(field, span - 1, 1) - 2.0 * field
    return field + wall_coef * wall_term + span_coef * span_term


def damping_rows(rows, total_rows):
    first = lax.axis_index("gy") * rows
    heights = (first + lax.broadcasted_iota(jnp.int32, (rows, 1), 0)).astype(F32)
    return jnp.exp(-wall_decay * heights / total_rows)


def matrix_kernel(stiffness, total_rows, coef_ref, target_ref, factor_ref, adj_down_ref, rims_ref, left_ref):
    planes, rows, span = target_ref.shape
    damping = damping_rows(rows, total_rows)
    factor = jnp.zeros((rows, span), F32)
    reduced = jnp.zeros((rows, span), F32)
    left = jnp.ones((rows, span), F32)
    for k in range(planes):
        diagonal = 1.0 + 2.0 * stiffness + coef_ref[k : k + 1, :] * damping
        factor = stiffness / (diagonal - stiffness * factor)
        reduced = (target_ref[k] + reduced) * factor
        left = left * factor
        factor_ref[k] = factor
        adj_down_ref[k] = reduced
        left_ref[k] = left
    value, right = reduced, factor
    rims_ref[1] = left
    rims_ref[2] = factor
    rims_ref[4] = reduced
    for k in range(planes - 2, -1, -1):
        factor = factor_ref[k]
        value = adj_down_ref[k] + factor * value
        left = left_ref[k] + factor * left
    rims_ref[0] = left
    rims_ref[3] = value


def velocity_kernel(velocity_ref, below_ref, above_ref, factor_ref, rims_ref, down_ref, send_ref):
    planes, rows, span = velocity_ref.shape
    reduced = jnp.zeros((rows, span), F32)
    for k in range(planes):
        forcing = explicit(velocity_ref[k], below_ref[k : k + 1, :], above_ref[k : k + 1, :])
        reduced = (forcing + reduced) * factor_ref[k]
        down_ref[k] = reduced
    value = reduced
    for k in range(planes - 2, -1, -1):
        value = down_ref[k] + factor_ref[k] * value
    parts = send_ref.shape[0]
    half = send_ref.shape[2]
    pieces = [rims_ref[i] for i in range(5)] + [value, reduced]
    for i, piece in enumerate(pieces):
        for j in range(parts):
            chunk, side = divmod(j, rows // half)
            send_ref[j, i] = piece[side * half : (side + 1) * half, chunk * LANES : (chunk + 1) * LANES]


def reduced_kernel(in_ref, out_ref, keep_ref):
    blocks = in_ref.shape[0]
    tile = in_ref.shape[2:]
    zero = jnp.zeros(tile, F32)
    gamma, beta_a, beta_v = zero, zero, zero
    for i in range(blocks):
        top, cross, low = in_ref[i, 0], in_ref[i, 1], in_ref[i, 2]
        top_a, low_a, top_v, low_v = in_ref[i, 3], in_ref[i, 4], in_ref[i, 5], in_ref[i, 6]
        inverse = 1.0 / (1.0 - top * gamma)
        tau_a = (top_a + top * beta_a) * inverse
        tau_v = (top_v + top * beta_v) * inverse
        sigma = cross * inverse
        keep_ref[i, 0] = tau_a
        keep_ref[i, 1] = tau_v
        keep_ref[i, 2] = sigma
        keep_ref[i, 3] = gamma
        keep_ref[i, 4] = beta_a
        keep_ref[i, 5] = beta_v
        beta_a = low_a + cross * (beta_a + gamma * tau_a)
        beta_v = low_v + cross * (beta_v + gamma * tau_v)
        gamma = low + cross * gamma * sigma
    next_a, next_v = zero, zero
    for i in range(blocks - 1, -1, -1):
        out_ref[i, 1] = next_a
        out_ref[i, 3] = next_v
        next_a = keep_ref[i, 0] + keep_ref[i, 2] * next_a
        next_v = keep_ref[i, 1] + keep_ref[i, 2] * next_v
        out_ref[i, 0] = keep_ref[i, 4] + keep_ref[i, 3] * next_a
        out_ref[i, 2] = keep_ref[i, 5] + keep_ref[i, 3] * next_v


def combine_kernel(
    stiffness, total_rows, factor_ref, adj_down_ref, down_ref, back_ref, map_ref,
    new_ref, adj_ref, sums_ref, low_ref, high_ref, left_ref,
):
    planes, rows, span = factor_ref.shape
    half = back_ref.shape[2]
    per = rows // half
    damping = damping_rows(rows, total_rows)
    scale = 1.0 / stiffness

    def assembled(i):
        return jnp.concatenate(
            [
                jnp.concatenate([back_ref[chunk * per + side, i] for side in range(per)], axis=0)
                for chunk in range(span // LANES)
            ],
            axis=1,
        )

    prev_a, value_a, prev_v, value_v = (assembled(i) for i in range(4))
    left = jnp.ones((rows, span), F32)
    for k in range(planes):
        left = left * factor_ref[k]
        left_ref[k] = left
    patch_rows, patch_lanes = sums_ref.shape
    row_ids = lax.broadcasted_iota(jnp.int32, (patch_rows, span), 0)
    lane_ids = lax.broadcasted_iota(jnp.int32, (patch_lanes, span), 0)
    total = jnp.zeros((3 * patch_rows, patch_lanes), F32)
    for k in range(planes - 1, -1, -1):
        factor, left = factor_ref[k], left_ref[k]
        value_a = adj_down_ref[k] + left * prev_a + factor * value_a
        value_v = down_ref[k] + left * prev_v + factor * value_v
        adjoint = value_a * scale
        new = value_v * scale
        adj_ref[k] = adjoint
        new_ref[k] = new
        low_ref[k : k + 1, :] = adjoint[:1]
        high_ref[k : k + 1, :] = adjoint[rows - 1 :]
        cells = jnp.sum(adjoint * new * damping, axis=0, keepdims=True)
        patches = map_ref[k : k + 1, :]
        first = cells.astype(jnp.bfloat16).astype(F32)
        rest = cells - first
        second = rest.astype(jnp.bfloat16).astype(F32)
        third = rest - second
        in_row = row_ids == patches // patch_lanes
        parts = jnp.concatenate(
            [jnp.where(in_row, part, 0.0) for part in (first, second, third)], axis=0
        ).astype(jnp.bfloat16)
        places = jnp.where(lane_ids == patches % patch_lanes, 1.0, 0.0).astype(jnp.bfloat16)
        total = total + lax.dot_general(
            parts, places, (((1,), (1,)), ((), ())), preferred_element_type=F32
        )
    sums_ref[...] = (
        total[:patch_rows] + total[patch_rows : 2 * patch_rows] + total[2 * patch_rows :]
    )


def gradient_kernel(adj_ref, below_ref, above_ref, out_ref):
    for k in range(adj_ref.shape[0]):
        out_ref[k] = explicit(adj_ref[k], below_ref[k : k + 1, :], above_ref[k : k + 1, :])


def call(kernel, outs, scratch, *operands):
    return pl.pallas_call(
        kernel,
        out_shape=outs,
        in_specs=[VMEM] * len(operands),
        out_specs=[VMEM] * len(outs),
        scratch_shapes=[pltpu.VMEM(dims, F32) for dims in scratch],
        compiler_params=pltpu.CompilerParams(vmem_limit_bytes=32 * 1024 * 1024),
    )(*operands)


def from_neighbours(low, high):
    count = lax.axis_size("gy")
    ends = count - 1
    below = lax.ppermute(high, "gy", [(i, i + 1) for i in range(ends)])
    above = lax.ppermute(low, "gy", [(i + 1, i) for i in range(ends)])
    return below, above


def local(velocity, cotangent, shape_coef, patch_map, broken):
    planes, rows, span = velocity.shape
    groups_x = lax.axis_size("gx")
    groups_y = lax.axis_size("gy")
    total_rows = rows * groups_y
    stiffness = 3.0 * planes * planes
    field = (planes, rows, span)
    half = rows * span // (groups_x * LANES)
    below, above = from_neighbours(velocity[:, 0], velocity[:, rows - 1])

    def with_sizes(kernel):
        return lambda *refs: kernel(stiffness, total_rows, *refs)

    factor, adj_down, rims = call(
        with_sizes(matrix_kernel),
        [shape_of(*field), shape_of(*field), shape_of(5, rows, span)],
        [field],
        shape_coef,
        cotangent,
    )
    down, send = call(
        velocity_kernel,
        [shape_of(*field), shape_of(groups_x, 7, half, LANES)],
        [],
        velocity,
        below,
        above,
        factor,
        rims,
    )
    blocks = lax.all_to_all(send, "gx", 0, 0, tiled=True)
    (solved,) = call(
        reduced_kernel,
        [shape_of(groups_x, 4, half, LANES)],
        [(groups_x, 6, half, LANES)],
        blocks,
    )
    back = lax.all_to_all(solved, "gx", 0, 0, tiled=True)
    owned_count = broken.shape[0]
    patch_count = owned_count * groups_x * groups_y
    new_velocity, adjoint, sums, low, high = call(
        with_sizes(combine_kernel),
        [
            shape_of(*field),
            shape_of(*field),
            shape_of(patch_count // LANES, LANES),
            shape_of(planes, span),
            shape_of(planes, span),
        ],
        [field],
        factor,
        adj_down,
        down,
        back,
        patch_map,
    )
    below, above = from_neighbours(low, high)
    shares = lax.all_to_all(
        sums.reshape(groups_x * groups_y, owned_count), ("gx", "gy"), 0, 0, tiled=True
    )
    own_patches = jnp.sum(shares, axis=0)
    (grad_velocity,) = call(gradient_kernel, [shape_of(*field)], [], adjoint, below, above)
    norm_factor = 1.0 / math.sqrt(planes * groups_x * total_rows * span / patch_count)
    keep = (1 - broken).astype(F32)
    patch_sens = -keep * norm_factor * own_patches
    return (new_velocity, grad_velocity, patch_sens)


def solution(mesh):
    return jax.shard_map(
        local,
        mesh=mesh,
        in_specs=(
            P("gx", "gy", None),
            P("gx", "gy", None),
            P("gx", None),
            P("gx", None),
            P(("gx", "gy")),
        ),
        out_specs=(P("gx", "gy", None), P("gx", "gy", None), P(("gx", "gy"))),
        check_vma=False,
    )
```

```python
import functools
import math

import jax
import jax.numpy as jnp
from jax import lax
from jax.experimental import pallas as pl
from jax.experimental.pallas import tpu as pltpu
from jax.sharding import PartitionSpec as P

wall_coef = 0.2
span_coef = 0.15
wall_decay = 8.0
VMEM = pl.BlockSpec(memory_space=pltpu.VMEM)
F32 = jnp.float32
LANES = 128


def shape_of(*dims):
    return jax.ShapeDtypeStruct(dims, F32)


def explicit(field, below, above):
    rows, span = field.shape
    row_ids = lax.broadcasted_iota(jnp.int32, (rows, span), 0)
    lower = jnp.where(row_ids == 0, below, pltpu.roll(field, 1, 0))
    upper = jnp.where(row_ids == rows - 1, above, pltpu.roll(field, rows - 1, 0))
    wall_term = upper + lower - 2.0 * field
    span_term = pltpu.roll(field, 1, 1) + pltpu.roll(field, span - 1, 1) - 2.0 * field
    return field + wall_coef * wall_term + span_coef * span_term


def edges(refs, k, field):
    first_ref, second_ref = refs
    rows = field.shape[0]
    even = lax.axis_index("gy") % 2 == 0
    low, high = field[:1], field[rows - 1 :]
    first_ref[k : k + 1, :] = jnp.where(even, high, low)
    second_ref[k : k + 1, :] = jnp.where(even, low, high)


def halo(first_ref, second_ref, k):
    position = lax.axis_index("gy")
    even = position % 2 == 0
    inner = (position > 0) & (position < lax.axis_size("gy") - 1)
    first = first_ref[k : k + 1, :]
    second = jnp.where(inner, second_ref[k : k + 1, :], 0.0)
    return jnp.where(even, second, first), jnp.where(even, first, second)


def pair_swap(first, second):
    count = lax.axis_size("gy")
    inner = [(i, i + 1 if i % 2 else i - 1) for i in range(1, count - 1)]
    ends = [(0, 0), (count - 1, count - 1)]
    return (
        lax.ppermute(first, "gy", [(i, i ^ 1) for i in range(count)]),
        lax.ppermute(second, "gy", inner + ends),
    )


def edge_kernel(velocity_ref, held_ref, first_ref, second_ref):
    for k in range(velocity_ref.shape[0]):
        held_ref[k] = velocity_ref[k]
        edges((first_ref, second_ref), k, velocity_ref[k])


def damping_rows(rows, total_rows):
    first = lax.axis_index("gy") * rows
    heights = (first + lax.broadcasted_iota(jnp.int32, (rows, 1), 0)).astype(F32)
    return jnp.exp(-wall_decay * heights / total_rows)


def matrix_kernel(stiffness, total_rows, coef_ref, target_ref, factor_ref, adj_down_ref, rims_ref, left_ref):
    planes, rows, span = target_ref.shape
    damping = damping_rows(rows, total_rows)
    factor = jnp.zeros((rows, span), F32)
    reduced = jnp.zeros((rows, span), F32)
    left = jnp.ones((rows, span), F32)
    for k in range(planes):
        diagonal = 1.0 + 2.0 * stiffness + coef_ref[k : k + 1, :] * damping
        factor = stiffness / (diagonal - stiffness * factor)
        reduced = (target_ref[k] + reduced) * factor
        left = left * factor
        factor_ref[k] = factor
        adj_down_ref[k] = reduced
        left_ref[k] = left
    value, right = reduced, factor
    rims_ref[1] = left
    rims_ref[2] = factor
    rims_ref[4] = reduced
    for k in range(planes - 2, -1, -1):
        factor = factor_ref[k]
        value = adj_down_ref[k] + factor * value
        left = left_ref[k] + factor * left
    rims_ref[0] = left
    rims_ref[3] = value


def velocity_kernel(velocity_ref, first_ref, second_ref, factor_ref, rims_ref, down_ref, send_ref):
    planes, rows, span = velocity_ref.shape
    reduced = jnp.zeros((rows, span), F32)
    for k in range(planes):
        forcing = explicit(velocity_ref[k], *halo(first_ref, second_ref, k))
        reduced = (forcing + reduced) * factor_ref[k]
        down_ref[k] = reduced
    value = reduced
    for k in range(planes - 2, -1, -1):
        value = down_ref[k] + factor_ref[k] * value
    parts = send_ref.shape[0]
    half = send_ref.shape[2]
    pieces = [rims_ref[i] for i in range(5)] + [value, reduced]
    for i, piece in enumerate(pieces):
        for j in range(parts):
            chunk, side = divmod(j, rows // half)
            send_ref[j, i] = piece[side * half : (side + 1) * half, chunk * LANES : (chunk + 1) * LANES]


def reduced_kernel(in_ref, out_ref, keep_ref):
    blocks = in_ref.shape[0]
    tile = in_ref.shape[2:]
    zero = jnp.zeros(tile, F32)
    gamma, beta_a, beta_v = zero, zero, zero
    for i in range(blocks):
        top, cross, low = in_ref[i, 0], in_ref[i, 1], in_ref[i, 2]
        top_a, low_a, top_v, low_v = in_ref[i, 3], in_ref[i, 4], in_ref[i, 5], in_ref[i, 6]
        inverse = 1.0 / (1.0 - top * gamma)
        tau_a = (top_a + top * beta_a) * inverse
        tau_v = (top_v + top * beta_v) * inverse
        sigma = cross * inverse
        keep_ref[i, 0] = tau_a
        keep_ref[i, 1] = tau_v
        keep_ref[i, 2] = sigma
        keep_ref[i, 3] = gamma
        keep_ref[i, 4] = beta_a
        keep_ref[i, 5] = beta_v
        beta_a = low_a + cross * (beta_a + gamma * tau_a)
        beta_v = low_v + cross * (beta_v + gamma * tau_v)
        gamma = low + cross * gamma * sigma
    next_a, next_v = zero, zero
    for i in range(blocks - 1, -1, -1):
        out_ref[i, 1] = next_a
        out_ref[i, 3] = next_v
        next_a = keep_ref[i, 0] + keep_ref[i, 2] * next_a
        next_v = keep_ref[i, 1] + keep_ref[i, 2] * next_v
        out_ref[i, 0] = keep_ref[i, 4] + keep_ref[i, 3] * next_a
        out_ref[i, 2] = keep_ref[i, 5] + keep_ref[i, 3] * next_v


def combine_kernel(
    patch_count, stiffness, total_rows, factor_ref, adj_down_ref, down_ref, back_ref, map_ref,
    new_ref, adj_ref, sums_ref, first_ref, second_ref, left_ref,
):
    planes, rows, span = factor_ref.shape
    half = back_ref.shape[2]
    per = rows // half
    damping = damping_rows(rows, total_rows)
    scale = 1.0 / stiffness

    def assembled(i):
        return jnp.concatenate(
            [
                jnp.concatenate([back_ref[chunk * per + side, i] for side in range(per)], axis=0)
                for chunk in range(span // LANES)
            ],
            axis=1,
        )

    prev_a, value_a, prev_v, value_v = (assembled(i) for i in range(4))
    left = jnp.ones((rows, span), F32)
    for k in range(planes):
        left = left * factor_ref[k]
        left_ref[k] = left
    patch_rows = 16
    patch_lanes = patch_count // patch_rows
    row_ids = lax.broadcasted_iota(jnp.int32, (patch_rows, span), 0)
    lane_ids = lax.broadcasted_iota(jnp.int32, (patch_lanes, span), 0)
    total = jnp.zeros((3 * patch_rows, patch_lanes), F32)
    for k in range(planes - 1, -1, -1):
        factor, left = factor_ref[k], left_ref[k]
        value_a = adj_down_ref[k] + left * prev_a + factor * value_a
        value_v = down_ref[k] + left * prev_v + factor * value_v
        adjoint = value_a * scale
        new = value_v * scale
        adj_ref[k] = adjoint
        new_ref[k] = new
        edges((first_ref, second_ref), k, adjoint)
        cells = jnp.sum(adjoint * new * damping, axis=0, keepdims=True)
        patches = map_ref[k : k + 1, :]
        first = cells.astype(jnp.bfloat16).astype(F32)
        rest = cells - first
        second = rest.astype(jnp.bfloat16).astype(F32)
        third = rest - second
        in_row = row_ids == patches // patch_lanes
        parts = jnp.concatenate(
            [jnp.where(in_row, part, 0.0) for part in (first, second, third)], axis=0
        ).astype(jnp.bfloat16)
        places = jnp.where(lane_ids == patches % patch_lanes, 1.0, 0.0).astype(jnp.bfloat16)
        total = total + lax.dot_general(
            parts, places, (((1,), (1,)), ((), ())), preferred_element_type=F32
        )
    sums = total[:patch_rows] + total[patch_rows : 2 * patch_rows] + total[2 * patch_rows :]
    merged = LANES // patch_lanes
    copies = sums_ref.shape[0] * LANES // patch_count
    for i in range(patch_rows // merged):
        row = jnp.concatenate([sums[i * merged + j : i * merged + j + 1] for j in range(merged)], axis=1)
        sums_ref[i * copies : (i + 1) * copies, :] = jnp.broadcast_to(row, (copies, LANES))


def gradient_kernel(
    norm_factor, adj_ref, new_in_ref, first_ref, second_ref, broken_ref, out_ref, new_ref, weight_ref
):
    for k in range(adj_ref.shape[0]):
        out_ref[k] = explicit(adj_ref[k], *halo(first_ref, second_ref, k))
        new_ref[k] = new_in_ref[k]
    weight_ref[...] = -(1 - broken_ref[...]).astype(F32) * norm_factor


def patch_kernel(shares_ref, weight_ref, out_ref):
    owned = weight_ref.shape[1]
    per_row = LANES // owned
    device = lax.axis_index("gx") * lax.axis_size("gy") + lax.axis_index("gy")
    total = jnp.sum(shares_ref[...], axis=0, keepdims=True)
    total = jnp.broadcast_to(total, (8, LANES))
    shift = lax.rem(LANES - owned * lax.rem(device, per_row), LANES)
    out_ref[...] = weight_ref[...] * pltpu.roll(total, shift, 1)[:1, :owned]


def call(kernel, outs, scratch, *operands, cost=None):
    return pl.pallas_call(
        kernel,
        out_shape=outs,
        in_specs=[VMEM] * len(operands),
        out_specs=[VMEM] * len(outs),
        scratch_shapes=scratch,
        cost_estimate=cost,
        compiler_params=pltpu.CompilerParams(vmem_limit_bytes=32 * 1024 * 1024),
    )(*operands)


def local(velocity, cotangent, shape_coef, patch_map, broken):
    planes, rows, span = velocity.shape
    groups_x = lax.axis_size("gx")
    groups_y = lax.axis_size("gy")
    total_rows = rows * groups_y
    stiffness = 3.0 * planes * planes
    field = (planes, rows, span)
    plane = (planes, span)
    half = rows * span // (groups_x * LANES)

    def with_sizes(kernel):
        return lambda *refs: kernel(stiffness, total_rows, *refs)

    velocity, first, second = call(
        edge_kernel, [shape_of(*field), shape_of(*plane), shape_of(*plane)], [], velocity
    )
    first, second = pair_swap(first, second)
    factor, adj_down, rims = call(
        with_sizes(matrix_kernel),
        [
            shape_of(*field),
            shape_of(*field),
            shape_of(5, rows, span),
        ],
        [pltpu.VMEM(field, F32)],
        shape_coef,
        cotangent,
    )
    down, send = call(
        velocity_kernel,
        [shape_of(*field), shape_of(groups_x, 7, half, LANES)],
        [],
        velocity,
        first,
        second,
        factor,
        rims,
    )
    blocks = lax.all_to_all(send, "gx", 0, 0, tiled=True)
    (solved,) = call(
        reduced_kernel,
        [shape_of(groups_x, 4, half, LANES)],
        [pltpu.VMEM((groups_x, 6, half, LANES), F32)],
        blocks,
    )
    back = lax.all_to_all(solved, "gx", 0, 0, tiled=True)
    owned = broken.shape[0]
    devices = groups_x * groups_y
    new, adjoint, sums, first, second = call(
        with_sizes(functools.partial(combine_kernel, owned * devices)),
        [
            shape_of(*field),
            shape_of(*field),
            shape_of(devices, LANES),
            shape_of(*plane),
            shape_of(*plane),
        ],
        [pltpu.VMEM(field, F32)],
        factor,
        adj_down,
        down,
        back,
        patch_map,
    )
    first, second = pair_swap(first, second)
    shares = lax.all_to_all(sums, ("gx", "gy"), 0, 0, tiled=True)
    norm_factor = 1.0 / math.sqrt(planes * groups_x * total_rows * span / (owned * devices))
    grad_velocity, new_velocity, weight = call(
        functools.partial(gradient_kernel, norm_factor),
        [shape_of(*field), shape_of(*field), shape_of(1, owned)],
        [],
        adjoint,
        new,
        first,
        second,
        broken.reshape(1, owned),
    )
    (patch_sens,) = call(patch_kernel, [shape_of(1, owned)], [], shares, weight)
    return (new_velocity, grad_velocity, patch_sens.reshape(owned))


def solution(mesh):
    return jax.shard_map(
        local,
        mesh=mesh,
        in_specs=(
            P("gx", "gy", None),
            P("gx", "gy", None),
            P("gx", None),
            P("gx", None),
            P(("gx", "gy")),
        ),
        out_specs=(P("gx", "gy", None), P("gx", "gy", None), P(("gx", "gy"))),
        check_vma=False,
    )
```

```python
import functools
import math

import jax
import jax.numpy as jnp
from jax import lax
from jax.experimental import pallas as pl
from jax.experimental.pallas import tpu as pltpu
from jax.sharding import PartitionSpec as P

wall_coef = 0.2
span_coef = 0.15
wall_decay = 8.0
VMEM = pl.BlockSpec(memory_space=pltpu.VMEM)
F32 = jnp.float32
LANES = 128


def shape_of(*dims):
    return jax.ShapeDtypeStruct(dims, F32)


def explicit(field, below, above):
    rows, span = field.shape
    row_ids = lax.broadcasted_iota(jnp.int32, (rows, span), 0)
    lower = jnp.where(row_ids == 0, below, pltpu.roll(field, 1, 0))
    upper = jnp.where(row_ids == rows - 1, above, pltpu.roll(field, rows - 1, 0))
    wall_term = upper + lower - 2.0 * field
    span_term = pltpu.roll(field, 1, 1) + pltpu.roll(field, span - 1, 1) - 2.0 * field
    return field + wall_coef * wall_term + span_coef * span_term


def edges(refs, k, field):
    first_ref, second_ref = refs
    rows = field.shape[0]
    even = lax.axis_index("gy") % 2 == 0
    low, high = field[:1], field[rows - 1 :]
    first_ref[k : k + 1, :] = jnp.where(even, high, low)
    second_ref[k : k + 1, :] = jnp.where(even, low, high)


def halo(first_ref, second_ref, k):
    position = lax.axis_index("gy")
    even = position % 2 == 0
    inner = (position > 0) & (position < lax.axis_size("gy") - 1)
    first = first_ref[k : k + 1, :]
    second = jnp.where(inner, second_ref[k : k + 1, :], 0.0)
    return jnp.where(even, second, first), jnp.where(even, first, second)


def pair_swap(first, second):
    count = lax.axis_size("gy")
    inner = [(i, i + 1 if i % 2 else i - 1) for i in range(1, count - 1)]
    ends = [(0, 0), (count - 1, count - 1)]
    return (
        lax.ppermute(first, "gy", [(i, i ^ 1) for i in range(count)]),
        lax.ppermute(second, "gy", inner + ends),
    )


def edge_kernel(velocity_ref, held_ref, first_ref, second_ref):
    for k in range(velocity_ref.shape[0]):
        held_ref[k] = velocity_ref[k]
        edges((first_ref, second_ref), k, velocity_ref[k])


def damping_rows(rows, total_rows):
    first = lax.axis_index("gy") * rows
    heights = (first + lax.broadcasted_iota(jnp.int32, (rows, 1), 0)).astype(F32)
    return jnp.exp(-wall_decay * heights / total_rows)


def matrix_kernel(stiffness, total_rows, coef_ref, target_ref, factor_ref, adj_down_ref, rims_ref, left_ref):
    planes, rows, span = target_ref.shape
    damping = damping_rows(rows, total_rows)
    factor = jnp.zeros((rows, span), F32)
    reduced = jnp.zeros((rows, span), F32)
    left = jnp.ones((rows, span), F32)
    for k in range(planes):
        diagonal = 1.0 + 2.0 * stiffness + coef_ref[k : k + 1, :] * damping
        factor = stiffness / (diagonal - stiffness * factor)
        reduced = (target_ref[k] + reduced) * factor
        left = left * factor
        factor_ref[k] = factor
        adj_down_ref[k] = reduced
        left_ref[k] = left
    value, right = reduced, factor
    rims_ref[1] = left
    rims_ref[2] = factor
    rims_ref[4] = reduced
    for k in range(planes - 2, -1, -1):
        factor = factor_ref[k]
        value = adj_down_ref[k] + factor * value
        left = left_ref[k] + factor * left
    rims_ref[0] = left
    rims_ref[3] = value


def velocity_kernel(velocity_ref, first_ref, second_ref, factor_ref, rims_ref, down_ref, mine_ref, give_ref):
    planes, rows, span = velocity_ref.shape
    reduced = jnp.zeros((rows, span), F32)
    for k in range(planes):
        forcing = explicit(velocity_ref[k], *halo(first_ref, second_ref, k))
        reduced = (forcing + reduced) * factor_ref[k]
        down_ref[k] = reduced
    value = reduced
    for k in range(planes - 2, -1, -1):
        value = down_ref[k] + factor_ref[k] * value
    pieces = [rims_ref[i] for i in range(5)] + [value, reduced]
    split(half_first(), pieces, mine_ref, give_ref)


def place():
    position = lax.axis_index("gx")
    return position % 2, position // 2


def split(first, pieces, mine_ref, give_ref):
    width = mine_ref.shape[2]
    for i, piece in enumerate(pieces):
        low, high = piece[:, :width], piece[:, width:]
        mine_ref[i] = jnp.where(first, low, high)
        give_ref[i] = jnp.where(first, high, low)


def joined(first, mine, other):
    return jnp.concatenate([jnp.where(first, mine, other), jnp.where(first, other, mine)], axis=1)


def merged(is_left, mine_ref, other_ref, tie_ref):
    left, right = [], []
    for i in range(7):
        mine, other = mine_ref[i], other_ref[i]
        left.append(jnp.where(is_left, mine, other))
        right.append(jnp.where(is_left, other, mine))
    top_l, cross_l, low_l, *sides_l = left
    top_r, cross_r, low_r, *sides_r = right
    inverse = 1.0 / (1.0 - low_l * top_r)
    to_left, to_right = cross_l * inverse, cross_r * inverse
    through_top, through_low = top_r * to_left, low_l * to_right
    tie_ref[0], tie_ref[1], tie_ref[2], tie_ref[3] = to_left, through_low, through_top, to_right
    block = [top_l + cross_l * through_top, cross_l * to_right, low_r + cross_r * through_low]
    for side in range(2):
        tops_l, lows_l = sides_l[2 * side], sides_l[2 * side + 1]
        tops_r, lows_r = sides_r[2 * side], sides_r[2 * side + 1]
        low = (lows_l + low_l * tops_r) * inverse
        top = (tops_r + top_r * lows_l) * inverse
        tie_ref[4 + 2 * side], tie_ref[5 + 2 * side] = low, top
        block += [tops_l + cross_l * top, lows_r + cross_r * low]
    return block


def untied(tie_ref, outer):
    inner = []
    for side in range(2):
        below, above = outer[2 * side], outer[2 * side + 1]
        low = tie_ref[4 + 2 * side] + tie_ref[0] * below + tie_ref[1] * above
        top = tie_ref[5 + 2 * side] + tie_ref[2] * below + tie_ref[3] * above
        inner.append((low, top))
    (low_a, top_a), (low_v, top_v) = inner
    return (
        [outer[0], top_a, outer[2], top_v],
        [low_a, outer[1], low_v, outer[3]],
    )


def chosen(is_left, pair):
    return [jnp.where(is_left, x, y) for x, y in zip(*pair)]


def half_first():
    core, chip = place()
    return (core + chip) % 2 == 0


def quarter_first():
    _, chip = place()
    return (chip + chip // 2) % 2 == 0


def core_kernel(mine_ref, got_ref, tie_ref, keep_ref, give_ref):
    core, _ = place()
    split(quarter_first(), merged(core == 0, mine_ref, got_ref, tie_ref), keep_ref, give_ref)


def chip_kernel(mine_ref, got_ref, tie_ref, block_ref):
    _, chip = place()
    for i, value in enumerate(merged(chip % 2 == 0, mine_ref, got_ref, tie_ref)):
        block_ref[i] = value


def four_kernel(mine_ref, got_ref, tie_ref, rim_ref):
    _, chip = place()
    top, _, low, *sides = merged(chip // 2 % 2 == 0, mine_ref, got_ref, tie_ref)
    is_left = chip < 4
    rim_ref[0] = jnp.where(is_left, low, top)
    rim_ref[1] = jnp.where(is_left, sides[1], sides[0])
    rim_ref[2] = jnp.where(is_left, sides[3], sides[2])


def middle_kernel(rim_ref, got_ref, four_tie_ref, chip_tie_ref, mine_ref, give_ref):
    _, chip = place()
    is_left = chip < 4
    rim, got = rim_ref[0], got_ref[0]
    inverse = 1.0 / (1.0 - rim * got)
    outer = []
    for side in (1, 2):
        across = (got_ref[side] + got * rim_ref[side]) * inverse
        outer += [jnp.where(is_left, 0.0, across), jnp.where(is_left, across, 0.0)]
    outer = chosen(chip // 2 % 2 == 0, untied(four_tie_ref, outer))
    left, right = untied(chip_tie_ref, outer)
    for i in range(4):
        mine_ref[i] = jnp.where(chip % 2 == 0, left[i], right[i])
        give_ref[i] = jnp.where(chip % 2 == 0, right[i], left[i])


def spread_kernel(part_ref, got_ref, tie_ref, mine_ref, give_ref):
    core, _ = place()
    first = quarter_first()
    outer = [joined(first, part_ref[i], got_ref[i]) for i in range(4)]
    left, right = untied(tie_ref, outer)
    for i in range(4):
        mine_ref[i] = jnp.where(core == 0, left[i], right[i])
        give_ref[i] = jnp.where(core == 0, right[i], left[i])


def swap(array, distance):
    pairs = [(i, i ^ distance) for i in range(lax.axis_size("gx"))]
    return lax.ppermute(array, "gx", pairs)


def line_ends(mine, give):
    rows, width = mine.shape[1:]
    half = width // 2
    got = swap(give, 1)
    core_tie, part, give = call(
        core_kernel,
        [shape_of(8, rows, width), shape_of(7, rows, half), shape_of(7, rows, half)],
        [],
        mine,
        got,
    )
    got = swap(give, 3)
    chip_tie, block = call(
        chip_kernel, [shape_of(8, rows, half), shape_of(7, rows, half)], [], part, got
    )
    got = swap(block, 7)
    four_tie, rim = call(
        four_kernel, [shape_of(8, rows, half), shape_of(3, rows, half)], [], block, got
    )
    got = swap(rim, 15)
    part, give = call(
        middle_kernel, [shape_of(4, rows, half)] * 2, [], rim, got, four_tie, chip_tie
    )
    got = swap(give, 3)
    mine, give = call(spread_kernel, [shape_of(4, rows, width)] * 2, [], part, got, core_tie)
    return mine, swap(give, 1)


def combine_kernel(
    patch_count, stiffness, total_rows, factor_ref, adj_down_ref, down_ref, mine_ref, got_ref, map_ref,
    new_ref, adj_ref, sums_ref, first_ref, second_ref, left_ref,
):
    planes, rows, span = factor_ref.shape
    damping = damping_rows(rows, total_rows)
    scale = 1.0 / stiffness

    prev_a, value_a, prev_v, value_v = (
        joined(half_first(), mine_ref[i], got_ref[i]) for i in range(4)
    )
    left = jnp.ones((rows, span), F32)
    for k in range(planes):
        left = left * factor_ref[k]
        left_ref[k] = left
    patch_rows = 16
    patch_lanes = patch_count // patch_rows
    row_ids = lax.broadcasted_iota(jnp.int32, (patch_rows, span), 0)
    lane_ids = lax.broadcasted_iota(jnp.int32, (patch_lanes, span), 0)
    total = jnp.zeros((3 * patch_rows, patch_lanes), F32)
    for k in range(planes - 1, -1, -1):
        factor, left = factor_ref[k], left_ref[k]
        value_a = adj_down_ref[k] + left * prev_a + factor * value_a
        value_v = down_ref[k] + left * prev_v + factor * value_v
        adjoint = value_a * scale
        new = value_v * scale
        adj_ref[k] = adjoint
        new_ref[k] = new
        edges((first_ref, second_ref), k, adjoint)
        cells = jnp.sum(adjoint * new * damping, axis=0, keepdims=True)
        patches = map_ref[k : k + 1, :]
        first = cells.astype(jnp.bfloat16).astype(F32)
        rest = cells - first
        second = rest.astype(jnp.bfloat16).astype(F32)
        third = rest - second
        in_row = row_ids == patches // patch_lanes
        parts = jnp.concatenate(
            [jnp.where(in_row, part, 0.0) for part in (first, second, third)], axis=0
        ).astype(jnp.bfloat16)
        places = jnp.where(lane_ids == patches % patch_lanes, 1.0, 0.0).astype(jnp.bfloat16)
        total = total + lax.dot_general(
            parts, places, (((1,), (1,)), ((), ())), preferred_element_type=F32
        )
    sums = total[:patch_rows] + total[patch_rows : 2 * patch_rows] + total[2 * patch_rows :]
    merged = LANES // patch_lanes
    copies = sums_ref.shape[0] * LANES // patch_count
    for i in range(patch_rows // merged):
        row = jnp.concatenate([sums[i * merged + j : i * merged + j + 1] for j in range(merged)], axis=1)
        sums_ref[i * copies : (i + 1) * copies, :] = jnp.broadcast_to(row, (copies, LANES))


def gradient_kernel(
    norm_factor, adj_ref, new_in_ref, first_ref, second_ref, broken_ref, out_ref, new_ref, weight_ref
):
    for k in range(adj_ref.shape[0]):
        out_ref[k] = explicit(adj_ref[k], *halo(first_ref, second_ref, k))
        new_ref[k] = new_in_ref[k]
    weight_ref[...] = -(1 - broken_ref[...]).astype(F32) * norm_factor


def patch_kernel(shares_ref, weight_ref, out_ref):
    owned = weight_ref.shape[1]
    per_row = LANES // owned
    device = lax.axis_index("gx") * lax.axis_size("gy") + lax.axis_index("gy")
    total = jnp.sum(shares_ref[...], axis=0, keepdims=True)
    total = jnp.broadcast_to(total, (8, LANES))
    shift = lax.rem(LANES - owned * lax.rem(device, per_row), LANES)
    out_ref[...] = weight_ref[...] * pltpu.roll(total, shift, 1)[:1, :owned]


def call(kernel, outs, scratch, *operands):
    return pl.pallas_call(
        kernel,
        out_shape=outs,
        in_specs=[VMEM] * len(operands),
        out_specs=[VMEM] * len(outs),
        scratch_shapes=scratch,
        compiler_params=pltpu.CompilerParams(vmem_limit_bytes=32 * 1024 * 1024),
    )(*operands)


def local(velocity, cotangent, shape_coef, patch_map, broken):
    planes, rows, span = velocity.shape
    groups_x = lax.axis_size("gx")
    groups_y = lax.axis_size("gy")
    total_rows = rows * groups_y
    stiffness = 3.0 * planes * planes
    field = (planes, rows, span)
    plane = (planes, span)

    def with_sizes(kernel):
        return lambda *refs: kernel(stiffness, total_rows, *refs)

    velocity, first, second = call(
        edge_kernel, [shape_of(*field), shape_of(*plane), shape_of(*plane)], [], velocity
    )
    first, second = pair_swap(first, second)
    factor, adj_down, rims = call(
        with_sizes(matrix_kernel),
        [
            shape_of(*field),
            shape_of(*field),
            shape_of(5, rows, span),
        ],
        [pltpu.VMEM(field, F32)],
        shape_coef,
        cotangent,
    )
    down, mine, give = call(
        velocity_kernel,
        [shape_of(*field)] + [shape_of(7, rows, span // 2)] * 2,
        [],
        velocity,
        first,
        second,
        factor,
        rims,
    )
    mine, got = line_ends(mine, give)
    owned = broken.shape[0]
    devices = groups_x * groups_y
    new, adjoint, sums, first, second = call(
        with_sizes(functools.partial(combine_kernel, owned * devices)),
        [
            shape_of(*field),
            shape_of(*field),
            shape_of(devices, LANES),
            shape_of(*plane),
            shape_of(*plane),
        ],
        [pltpu.VMEM(field, F32)],
        factor,
        adj_down,
        down,
        mine,
        got,
        patch_map,
    )
    first, second = pair_swap(first, second)
    shares = lax.all_to_all(sums, ("gx", "gy"), 0, 0, tiled=True)
    norm_factor = 1.0 / math.sqrt(planes * groups_x * total_rows * span / (owned * devices))
    grad_velocity, new_velocity, weight = call(
        functools.partial(gradient_kernel, norm_factor),
        [shape_of(*field), shape_of(*field), shape_of(1, owned)],
        [],
        adjoint,
        new,
        first,
        second,
        broken.reshape(1, owned),
    )
    (patch_sens,) = call(patch_kernel, [shape_of(1, owned)], [], shares, weight)
    return (new_velocity, grad_velocity, patch_sens.reshape(owned))


def solution(mesh):
    return jax.shard_map(
        local,
        mesh=mesh,
        in_specs=(
            P("gx", "gy", None),
            P("gx", "gy", None),
            P("gx", None),
            P("gx", None),
            P(("gx", "gy")),
        ),
        out_specs=(P("gx", "gy", None), P("gx", "gy", None), P(("gx", "gy"))),
        check_vma=False,
    )
```

```python
import functools
import math

import jax
import jax.numpy as jnp
from jax import lax
from jax.experimental import pallas as pl
from jax.experimental.pallas import tpu as pltpu
from jax.sharding import PartitionSpec as P

wall_coef = 0.2
span_coef = 0.15
wall_decay = 8.0
VMEM = pl.BlockSpec(memory_space=pltpu.VMEM)
F32 = jnp.float32
LANES = 128
PATCH_ROWS = 16


def shape_of(*dims):
    return jax.ShapeDtypeStruct(dims, F32)


def explicit(field, below, above):
    rows, span = field.shape
    row_ids = lax.broadcasted_iota(jnp.int32, (rows, span), 0)
    lower = jnp.where(row_ids == 0, below, pltpu.roll(field, 1, 0))
    upper = jnp.where(row_ids == rows - 1, above, pltpu.roll(field, rows - 1, 0))
    wall_term = upper + lower - 2.0 * field
    span_term = pltpu.roll(field, 1, 1) + pltpu.roll(field, span - 1, 1) - 2.0 * field
    return field + wall_coef * wall_term + span_coef * span_term


def edges(refs, k, field):
    first_ref, second_ref = refs
    rows = field.shape[0]
    even = lax.axis_index("gy") % 2 == 0
    low, high = field[:1], field[rows - 1 :]
    first_ref[k : k + 1, :] = jnp.where(even, high, low)
    second_ref[k : k + 1, :] = jnp.where(even, low, high)


def halo(first_ref, second_ref, k):
    position = lax.axis_index("gy")
    even = position % 2 == 0
    inner = (position > 0) & (position < lax.axis_size("gy") - 1)
    first = first_ref[k : k + 1, :]
    second = jnp.where(inner, second_ref[k : k + 1, :], 0.0)
    return jnp.where(even, second, first), jnp.where(even, first, second)


def near_swap(edge):
    return lax.ppermute(edge, "gy", [(i, i ^ 1) for i in range(lax.axis_size("gy"))])


def far_swap(edge):
    count_x, count = lax.axis_size("gx"), lax.axis_size("gy")
    pairs = []
    for i in range(count_x):
        for j in range(count):
            target = j + 1 if j % 2 else j - 1
            inside = 0 <= target < count
            pairs.append((i * count + j, i * count + target if inside else (i ^ 1) * count + j))
    return lax.ppermute(edge, ("gx", "gy"), pairs)


def pair_swap(first, second):
    return near_swap(first), far_swap(second)


def edge_kernel(velocity_ref, held_ref, first_ref, second_ref):
    for k in range(velocity_ref.shape[0]):
        held_ref[k] = velocity_ref[k]
        edges((first_ref, second_ref), k, velocity_ref[k])


def damping_rows(rows, total_rows):
    first = lax.axis_index("gy") * rows
    heights = (first + lax.broadcasted_iota(jnp.int32, (rows, 1), 0)).astype(F32)
    return jnp.exp(-wall_decay * heights / total_rows)


def matrix_kernel(stiffness, total_rows, coef_ref, target_ref, factor_ref, adj_down_ref, left_ref, rims_ref):
    planes, rows, span = target_ref.shape
    damping = damping_rows(rows, total_rows)
    factor = jnp.zeros((rows, span), F32)
    reduced = jnp.zeros((rows, span), F32)
    left = jnp.ones((rows, span), F32)
    for k in range(planes):
        diagonal = 1.0 + 2.0 * stiffness + coef_ref[k : k + 1, :] * damping
        factor = stiffness / (diagonal - stiffness * factor)
        reduced = (target_ref[k] + reduced) * factor
        left = left * factor
        factor_ref[k] = factor
        adj_down_ref[k] = reduced
        left_ref[k] = left
    value, right = reduced, factor
    rims_ref[1] = left
    rims_ref[2] = factor
    rims_ref[4] = reduced
    for k in range(planes - 2, -1, -1):
        factor = factor_ref[k]
        value = adj_down_ref[k] + factor * value
        left = left_ref[k] + factor * left
    rims_ref[0] = left
    rims_ref[3] = value


def velocity_kernel(velocity_ref, second_ref, first_ref, factor_ref, rims_ref, down_ref, mine_ref, give_ref):
    planes, rows, span = velocity_ref.shape
    reduced = jnp.zeros((rows, span), F32)
    for k in range(planes):
        forcing = explicit(velocity_ref[k], *halo(first_ref, second_ref, k))
        reduced = (forcing + reduced) * factor_ref[k]
        down_ref[k] = reduced
    value = reduced
    for k in range(planes - 2, -1, -1):
        value = down_ref[k] + factor_ref[k] * value
    pieces = [rims_ref[i] for i in range(5)] + [value, reduced]
    split(half_first(), pieces, mine_ref, give_ref)


def place():
    position = lax.axis_index("gx")
    return position % 2, position // 2


def split(first, pieces, mine_ref, give_ref):
    width = mine_ref.shape[2]
    for i, piece in enumerate(pieces):
        low, high = piece[:, :width], piece[:, width:]
        mine_ref[i] = jnp.where(first, low, high)
        give_ref[i] = jnp.where(first, high, low)


def joined(first, mine, other):
    return jnp.concatenate([jnp.where(first, mine, other), jnp.where(first, other, mine)], axis=1)


def merged(is_left, mine_ref, other_ref, tie_ref):
    left, right = [], []
    for i in range(7):
        mine, other = mine_ref[i], other_ref[i]
        left.append(jnp.where(is_left, mine, other))
        right.append(jnp.where(is_left, other, mine))
    top_l, cross_l, low_l, *sides_l = left
    top_r, cross_r, low_r, *sides_r = right
    inverse = 1.0 / (1.0 - low_l * top_r)
    to_left, to_right = cross_l * inverse, cross_r * inverse
    through_top, through_low = top_r * to_left, low_l * to_right
    tie_ref[0], tie_ref[1], tie_ref[2], tie_ref[3] = to_left, through_low, through_top, to_right
    block = [top_l + cross_l * through_top, cross_l * to_right, low_r + cross_r * through_low]
    for side in range(2):
        tops_l, lows_l = sides_l[2 * side], sides_l[2 * side + 1]
        tops_r, lows_r = sides_r[2 * side], sides_r[2 * side + 1]
        low = (lows_l + low_l * tops_r) * inverse
        top = (tops_r + top_r * lows_l) * inverse
        tie_ref[4 + 2 * side], tie_ref[5 + 2 * side] = low, top
        block += [tops_l + cross_l * top, lows_r + cross_r * low]
    return block


def untied(tie_ref, outer):
    inner = []
    for side in range(2):
        below, above = outer[2 * side], outer[2 * side + 1]
        low = tie_ref[4 + 2 * side] + tie_ref[0] * below + tie_ref[1] * above
        top = tie_ref[5 + 2 * side] + tie_ref[2] * below + tie_ref[3] * above
        inner.append((low, top))
    (low_a, top_a), (low_v, top_v) = inner
    return (
        [outer[0], top_a, outer[2], top_v],
        [low_a, outer[1], low_v, outer[3]],
    )


def chosen(is_left, pair):
    return [jnp.where(is_left, x, y) for x, y in zip(*pair)]


def half_first():
    core, chip = place()
    return (core + chip) % 2 == 0


def quarter_first():
    _, chip = place()
    return (chip + chip // 2) % 2 == 0


def core_kernel(mine_ref, got_ref, tie_ref, keep_ref, give_ref):
    core, _ = place()
    split(quarter_first(), merged(core == 0, mine_ref, got_ref, tie_ref), keep_ref, give_ref)


def chip_kernel(mine_ref, got_ref, tie_ref, block_ref):
    _, chip = place()
    for i, value in enumerate(merged(chip % 2 == 0, mine_ref, got_ref, tie_ref)):
        block_ref[i] = value


def four_kernel(mine_ref, got_ref, tie_ref, rim_ref):
    _, chip = place()
    top, _, low, *sides = merged(chip // 2 % 2 == 0, mine_ref, got_ref, tie_ref)
    is_left = chip < 4
    rim_ref[0] = jnp.where(is_left, low, top)
    rim_ref[1] = jnp.where(is_left, sides[1], sides[0])
    rim_ref[2] = jnp.where(is_left, sides[3], sides[2])


def middle_kernel(rim_ref, got_ref, four_tie_ref, chip_tie_ref, mine_ref, give_ref):
    _, chip = place()
    is_left = chip < 4
    rim, got = rim_ref[0], got_ref[0]
    inverse = 1.0 / (1.0 - rim * got)
    outer = []
    for side in (1, 2):
        across = (got_ref[side] + got * rim_ref[side]) * inverse
        outer += [jnp.where(is_left, 0.0, across), jnp.where(is_left, across, 0.0)]
    outer = chosen(chip // 2 % 2 == 0, untied(four_tie_ref, outer))
    left, right = untied(chip_tie_ref, outer)
    for i in range(4):
        mine_ref[i] = jnp.where(chip % 2 == 0, left[i], right[i])
        give_ref[i] = jnp.where(chip % 2 == 0, right[i], left[i])


def spread_kernel(part_ref, got_ref, tie_ref, mine_ref, give_ref):
    core, _ = place()
    first = quarter_first()
    outer = [joined(first, part_ref[i], got_ref[i]) for i in range(4)]
    left, right = untied(tie_ref, outer)
    for i in range(4):
        mine_ref[i] = jnp.where(core == 0, left[i], right[i])
        give_ref[i] = jnp.where(core == 0, right[i], left[i])


def swap(array, distance):
    pairs = [(i, i ^ distance) for i in range(lax.axis_size("gx"))]
    return lax.ppermute(array, "gx", pairs)


def line_ends(mine, give):
    rows, width = mine.shape[1:]
    half = width // 2
    got = swap(give, 1)
    core_tie, part, give = call(
        core_kernel,
        [shape_of(8, rows, width), shape_of(7, rows, half), shape_of(7, rows, half)],
        [],
        mine,
        got,
    )
    got = swap(give, 3)
    chip_tie, block = call(
        chip_kernel, [shape_of(8, rows, half), shape_of(7, rows, half)], [], part, got
    )
    got = swap(block, 7)
    four_tie, rim = call(
        four_kernel, [shape_of(8, rows, half), shape_of(3, rows, half)], [], block, got
    )
    got = swap(rim, 15)
    part, give = call(
        middle_kernel, [shape_of(4, rows, half)] * 2, [], rim, got, four_tie, chip_tie
    )
    got = swap(give, 3)
    return call(spread_kernel, [shape_of(4, rows, width)] * 2, [], part, got, core_tie)


def lanes_of(is_mine, width):
    first = half_first() if is_mine else jnp.logical_not(half_first())
    return pl.ds(pl.multiple_of(jnp.where(first, 0, width), LANES), width)


def back_sweep(lanes, factor_ref, left_ref, down_ref, below, above, scale, out_ref):
    value = above
    for k in range(out_ref.shape[0] - 1, -1, -1):
        value = down_ref[k, :, lanes] + left_ref[k, :, lanes] * below + factor_ref[k, :, lanes] * value
        out_ref[k] = value * scale


def patch_sums(patch_count, total_rows, lanes, map_ref, adj_ref, new_ref):
    planes, rows, width = adj_ref.shape
    damping = damping_rows(rows, total_rows)
    patch_rows = PATCH_ROWS
    patch_lanes = patch_count // patch_rows
    row_ids = lax.broadcasted_iota(jnp.int32, (patch_rows, width), 0)
    lane_ids = lax.broadcasted_iota(jnp.int32, (patch_lanes, width), 0)
    total = jnp.zeros((3 * patch_rows, patch_lanes), F32)
    for k in range(planes):
        cells = jnp.sum(adj_ref[k] * new_ref[k] * damping, axis=0, keepdims=True)
        patches = map_ref[k : k + 1, lanes]
        first = cells.astype(jnp.bfloat16).astype(F32)
        rest = cells - first
        second = rest.astype(jnp.bfloat16).astype(F32)
        third = rest - second
        in_row = row_ids == patches // patch_lanes
        parts = jnp.concatenate(
            [jnp.where(in_row, part, 0.0) for part in (first, second, third)], axis=0
        ).astype(jnp.bfloat16)
        places = jnp.where(lane_ids == patches % patch_lanes, 1.0, 0.0).astype(jnp.bfloat16)
        total = total + lax.dot_general(
            parts, places, (((1,), (1,)), ((), ())), preferred_element_type=F32
        )
    return total[:patch_rows] + total[patch_rows : 2 * patch_rows] + total[2 * patch_rows :]


def own_half_kernel(
    patch_count, stiffness, total_rows, factor_ref, left_ref, adj_down_ref, down_ref, ends_ref, map_ref,
    adj_ref, new_ref, sums_ref,
):
    lanes = lanes_of(True, adj_ref.shape[2])
    sweep = (lanes, factor_ref, left_ref)
    back_sweep(*sweep, adj_down_ref, ends_ref[0], ends_ref[1], 1.0 / stiffness, adj_ref)
    back_sweep(*sweep, down_ref, ends_ref[2], ends_ref[3], 1.0 / stiffness, new_ref)
    sums_ref[...] = patch_sums(patch_count, total_rows, lanes, map_ref, adj_ref, new_ref)


def adjoint_kernel(
    stiffness, total_rows, factor_ref, left_ref, adj_down_ref, ends_ref, mine_ref,
    adj_ref, first_ref, second_ref,
):
    lanes = lanes_of(False, adj_ref.shape[2])
    back_sweep(
        lanes, factor_ref, left_ref, adj_down_ref, ends_ref[0], ends_ref[1], 1.0 / stiffness, adj_ref
    )
    for k in range(adj_ref.shape[0]):
        edges((first_ref, second_ref), k, joined(half_first(), mine_ref[k], adj_ref[k]))


def shares_kernel(
    patch_count, stiffness, total_rows, factor_ref, left_ref, down_ref, ends_ref, map_ref, adj_ref, mine_ref,
    new_ref, shares_ref,
):
    lanes = lanes_of(False, adj_ref.shape[2])
    back_sweep(
        lanes, factor_ref, left_ref, down_ref, ends_ref[2], ends_ref[3], 1.0 / stiffness, new_ref
    )
    sums = mine_ref[...] + patch_sums(patch_count, total_rows, lanes, map_ref, adj_ref, new_ref)
    patch_rows, patch_lanes = sums.shape
    merged_rows = LANES // patch_lanes
    copies = shares_ref.shape[0] * LANES // patch_count
    for i in range(patch_rows // merged_rows):
        row = jnp.concatenate(
            [sums[i * merged_rows + j : i * merged_rows + j + 1] for j in range(merged_rows)], axis=1
        )
        shares_ref[i * copies : (i + 1) * copies, :] = jnp.broadcast_to(row, (copies, LANES))


def gradient_kernel(
    norm_factor, adj_ref, adj_got_ref, new_in_ref, new_got_ref, second_ref, first_ref, broken_ref,
    out_ref, new_ref, weight_ref,
):
    for k in range(adj_ref.shape[0]):
        adjoint = joined(half_first(), adj_ref[k], adj_got_ref[k])
        out_ref[k] = explicit(adjoint, *halo(first_ref, second_ref, k))
        new_ref[k] = joined(half_first(), new_in_ref[k], new_got_ref[k])
    weight_ref[...] = -(1 - broken_ref[...]).astype(F32) * norm_factor


def patch_kernel(shares_ref, weight_ref, out_ref):
    owned = weight_ref.shape[1]
    per_row = LANES // owned
    device = lax.axis_index("gx") * lax.axis_size("gy") + lax.axis_index("gy")
    total = jnp.sum(shares_ref[...], axis=0, keepdims=True)
    total = jnp.broadcast_to(total, (8, LANES))
    shift = lax.rem(LANES - owned * lax.rem(device, per_row), LANES)
    out_ref[...] = weight_ref[...] * pltpu.roll(total, shift, 1)[:1, :owned]


def call(kernel, outs, scratch, *operands):
    return pl.pallas_call(
        kernel,
        out_shape=outs,
        in_specs=[VMEM] * len(operands),
        out_specs=[VMEM] * len(outs),
        scratch_shapes=scratch,
        compiler_params=pltpu.CompilerParams(vmem_limit_bytes=32 * 1024 * 1024),
    )(*operands)


def local(velocity, cotangent, shape_coef, patch_map, broken):
    planes, rows, span = velocity.shape
    groups_x = lax.axis_size("gx")
    groups_y = lax.axis_size("gy")
    total_rows = rows * groups_y
    stiffness = 3.0 * planes * planes
    field = (planes, rows, span)
    plane = (planes, span)

    def with_sizes(kernel):
        return lambda *refs: kernel(stiffness, total_rows, *refs)

    velocity, first, second = call(
        edge_kernel, [shape_of(*field), shape_of(*plane), shape_of(*plane)], [], velocity
    )
    first, second = pair_swap(first, second)
    factor, adj_down, left, rims = call(
        with_sizes(matrix_kernel),
        [shape_of(*field)] * 3 + [shape_of(5, rows, span)],
        [],
        shape_coef,
        cotangent,
    )
    down, mine, give = call(
        velocity_kernel,
        [shape_of(*field)] + [shape_of(7, rows, span // 2)] * 2,
        [],
        velocity,
        second,
        first,
        factor,
        rims,
    )
    mine, give = line_ends(mine, give)
    got = swap(give, 1)
    owned = broken.shape[0]
    devices = groups_x * groups_y
    patch_count = owned * devices
    half = (planes, rows, span // 2)
    adj_mine, new_mine, sums = call(
        with_sizes(functools.partial(own_half_kernel, patch_count)),
        [shape_of(*half), shape_of(*half), shape_of(PATCH_ROWS, patch_count // PATCH_ROWS)],
        [],
        factor,
        left,
        adj_down,
        down,
        mine,
        patch_map,
    )
    adj_got, first, second = call(
        with_sizes(adjoint_kernel),
        [shape_of(*half), shape_of(*plane), shape_of(*plane)],
        [],
        factor,
        left,
        adj_down,
        got,
        adj_mine,
    )
    first, second = pair_swap(first, second)
    new_got, sums = call(
        with_sizes(functools.partial(shares_kernel, patch_count)),
        [shape_of(*half), shape_of(devices, LANES)],
        [],
        factor,
        left,
        down,
        got,
        patch_map,
        adj_got,
        sums,
    )
    shares = lax.all_to_all(sums, ("gx", "gy"), 0, 0, tiled=True)
    norm_factor = 1.0 / math.sqrt(planes * groups_x * total_rows * span / (owned * devices))
    grad_velocity, new_velocity, weight = call(
        functools.partial(gradient_kernel, norm_factor),
        [shape_of(*field), shape_of(*field), shape_of(1, owned)],
        [],
        adj_mine,
        adj_got,
        new_mine,
        new_got,
        second,
        first,
        broken.reshape(1, owned),
    )
    (patch_sens,) = call(patch_kernel, [shape_of(1, owned)], [], shares, weight)
    return (new_velocity, grad_velocity, patch_sens.reshape(owned))


def solution(mesh):
    return jax.shard_map(
        local,
        mesh=mesh,
        in_specs=(
            P("gx", "gy", None),
            P("gx", "gy", None),
            P("gx", None),
            P("gx", None),
            P(("gx", "gy")),
        ),
        out_specs=(P("gx", "gy", None), P("gx", "gy", None), P(("gx", "gy"))),
        check_vma=False,
    )
```

```python
import functools
import math

import jax
import jax.numpy as jnp
from jax import lax
from jax.experimental import pallas as pl
from jax.experimental.pallas import tpu as pltpu
from jax.sharding import PartitionSpec as P

wall_coef = 0.2
span_coef = 0.15
wall_decay = 8.0
VMEM = pl.BlockSpec(memory_space=pltpu.VMEM)
F32 = jnp.float32
LANES = 128
PATCH_ROWS = 16


def shape_of(*dims):
    return jax.ShapeDtypeStruct(dims, F32)


def explicit(field, below, above):
    rows, span = field.shape
    row_ids = lax.broadcasted_iota(jnp.int32, (rows, span), 0)
    lower = jnp.where(row_ids == 0, below, pltpu.roll(field, 1, 0))
    upper = jnp.where(row_ids == rows - 1, above, pltpu.roll(field, rows - 1, 0))
    wall_term = upper + lower - 2.0 * field
    span_term = pltpu.roll(field, 1, 1) + pltpu.roll(field, span - 1, 1) - 2.0 * field
    return field + wall_coef * wall_term + span_coef * span_term


def edges(refs, k, field):
    first_ref, second_ref = refs
    rows = field.shape[0]
    even = lax.axis_index("gy") % 2 == 0
    low, high = field[:1], field[rows - 1 :]
    first_ref[k : k + 1, :] = jnp.where(even, high, low)
    second_ref[k : k + 1, :] = jnp.where(even, low, high)


def halo(first_ref, second_ref, k):
    position = lax.axis_index("gy")
    even = position % 2 == 0
    inner = (position > 0) & (position < lax.axis_size("gy") - 1)
    first = first_ref[k : k + 1, :]
    second = jnp.where(inner, second_ref[k : k + 1, :], 0.0)
    return jnp.where(even, second, first), jnp.where(even, first, second)


def near_swap(edge):
    return lax.ppermute(edge, "gy", [(i, i ^ 1) for i in range(lax.axis_size("gy"))])


def far_swap(edge):
    count_x, count = lax.axis_size("gx"), lax.axis_size("gy")
    pairs = []
    for i in range(count_x):
        for j in range(count):
            target = j + 1 if j % 2 else j - 1
            inside = 0 <= target < count
            pairs.append((i * count + j, i * count + target if inside else (i ^ 1) * count + j))
    return lax.ppermute(edge, ("gx", "gy"), pairs)


def pair_swap(first, second):
    return near_swap(first), far_swap(second)


def edge_kernel(velocity_ref, held_ref, first_ref, second_ref):
    for k in range(velocity_ref.shape[0]):
        held_ref[k] = velocity_ref[k]
        edges((first_ref, second_ref), k, velocity_ref[k])


def damping_rows(rows, total_rows):
    first = lax.axis_index("gy") * rows
    heights = (first + lax.broadcasted_iota(jnp.int32, (rows, 1), 0)).astype(F32)
    return jnp.exp(-wall_decay * heights / total_rows)


def matrix_kernel(stiffness, total_rows, coef_ref, target_ref, factor_ref, adj_down_ref, left_ref, rims_ref):
    planes, rows, span = target_ref.shape
    damping = damping_rows(rows, total_rows)
    factor = jnp.zeros((rows, span), F32)
    reduced = jnp.zeros((rows, span), F32)
    left = jnp.ones((rows, span), F32)
    for k in range(planes):
        diagonal = 1.0 + 2.0 * stiffness + coef_ref[k : k + 1, :] * damping
        factor = stiffness / (diagonal - stiffness * factor)
        reduced = (target_ref[k] + reduced) * factor
        left = left * factor
        factor_ref[k] = factor
        adj_down_ref[k] = reduced
        left_ref[k] = left
    value, right = reduced, factor
    rims_ref[1] = left
    rims_ref[2] = factor
    rims_ref[4] = reduced
    for k in range(planes - 2, -1, -1):
        factor = factor_ref[k]
        value = adj_down_ref[k] + factor * value
        left = left_ref[k] + factor * left
    rims_ref[0] = left
    rims_ref[3] = value


def velocity_kernel(velocity_ref, second_ref, first_ref, factor_ref, rims_ref, down_ref, mine_ref, give_ref):
    planes, rows, span = velocity_ref.shape
    reduced = jnp.zeros((rows, span), F32)
    for k in range(planes):
        forcing = explicit(velocity_ref[k], *halo(first_ref, second_ref, k))
        reduced = (forcing + reduced) * factor_ref[k]
        down_ref[k] = reduced
    value = reduced
    for k in range(planes - 2, -1, -1):
        value = down_ref[k] + factor_ref[k] * value
    pieces = [rims_ref[i] for i in range(5)] + [value, reduced]
    split(half_first(), pieces, mine_ref, give_ref)


def place():
    position = lax.axis_index("gx")
    return position % 2, position // 2


def split(first, pieces, mine_ref, give_ref):
    width = mine_ref.shape[2]
    for i, piece in enumerate(pieces):
        low, high = piece[:, :width], piece[:, width:]
        mine_ref[i] = jnp.where(first, low, high)
        give_ref[i] = jnp.where(first, high, low)


def joined(first, mine, other):
    return jnp.concatenate([jnp.where(first, mine, other), jnp.where(first, other, mine)], axis=1)


def merged(is_left, mine_ref, other_ref, tie_ref):
    left, right = [], []
    for i in range(7):
        mine, other = mine_ref[i], other_ref[i]
        left.append(jnp.where(is_left, mine, other))
        right.append(jnp.where(is_left, other, mine))
    top_l, cross_l, low_l, *sides_l = left
    top_r, cross_r, low_r, *sides_r = right
    inverse = 1.0 / (1.0 - low_l * top_r)
    to_left, to_right = cross_l * inverse, cross_r * inverse
    through_top, through_low = top_r * to_left, low_l * to_right
    tie_ref[0], tie_ref[1], tie_ref[2], tie_ref[3] = to_left, through_low, through_top, to_right
    block = [top_l + cross_l * through_top, cross_l * to_right, low_r + cross_r * through_low]
    for side in range(2):
        tops_l, lows_l = sides_l[2 * side], sides_l[2 * side + 1]
        tops_r, lows_r = sides_r[2 * side], sides_r[2 * side + 1]
        low = (lows_l + low_l * tops_r) * inverse
        top = (tops_r + top_r * lows_l) * inverse
        tie_ref[4 + 2 * side], tie_ref[5 + 2 * side] = low, top
        block += [tops_l + cross_l * top, lows_r + cross_r * low]
    return block


def untied(tie_ref, outer):
    inner = []
    for side in range(2):
        below, above = outer[2 * side], outer[2 * side + 1]
        low = tie_ref[4 + 2 * side] + tie_ref[0] * below + tie_ref[1] * above
        top = tie_ref[5 + 2 * side] + tie_ref[2] * below + tie_ref[3] * above
        inner.append((low, top))
    (low_a, top_a), (low_v, top_v) = inner
    return (
        [outer[0], top_a, outer[2], top_v],
        [low_a, outer[1], low_v, outer[3]],
    )


def chosen(is_left, pair):
    return [jnp.where(is_left, x, y) for x, y in zip(*pair)]


def half_first():
    core, chip = place()
    return (core + chip) % 2 == 0


def quarter_first():
    _, chip = place()
    return (chip + chip // 2) % 2 == 0


def core_kernel(mine_ref, got_ref, tie_ref, keep_ref, give_ref):
    core, _ = place()
    split(quarter_first(), merged(core == 0, mine_ref, got_ref, tie_ref), keep_ref, give_ref)


def chip_kernel(mine_ref, got_ref, tie_ref, block_ref):
    _, chip = place()
    for i, value in enumerate(merged(chip % 2 == 0, mine_ref, got_ref, tie_ref)):
        block_ref[i] = value


def four_kernel(mine_ref, got_ref, tie_ref, rim_ref):
    _, chip = place()
    top, _, low, *sides = merged(chip // 2 % 2 == 0, mine_ref, got_ref, tie_ref)
    is_left = chip < 4
    rim_ref[0] = jnp.where(is_left, low, top)
    rim_ref[1] = jnp.where(is_left, sides[1], sides[0])
    rim_ref[2] = jnp.where(is_left, sides[3], sides[2])


def middle_kernel(rim_ref, got_ref, four_tie_ref, chip_tie_ref, mine_ref, give_ref):
    _, chip = place()
    is_left = chip < 4
    rim, got = rim_ref[0], got_ref[0]
    inverse = 1.0 / (1.0 - rim * got)
    outer = []
    for side in (1, 2):
        across = (got_ref[side] + got * rim_ref[side]) * inverse
        outer += [jnp.where(is_left, 0.0, across), jnp.where(is_left, across, 0.0)]
    outer = chosen(chip // 2 % 2 == 0, untied(four_tie_ref, outer))
    left, right = untied(chip_tie_ref, outer)
    for i in range(4):
        mine_ref[i] = jnp.where(chip % 2 == 0, left[i], right[i])
        give_ref[i] = jnp.where(chip % 2 == 0, right[i], left[i])


def spread_kernel(low_part_ref, low_got_ref, high_part_ref, high_got_ref, tie_ref, mine_ref, give_ref):
    core, chip = place()
    first = quarter_first()
    is_low = chip < 4
    outer = [
        joined(
            first,
            jnp.where(is_low, low_part_ref[i], high_part_ref[i]),
            jnp.where(is_low, low_got_ref[i], high_got_ref[i]),
        )
        for i in range(4)
    ]
    left, right = untied(tie_ref, outer)
    for i in range(4):
        mine_ref[i] = jnp.where(core == 0, left[i], right[i])
        give_ref[i] = jnp.where(core == 0, right[i], left[i])


def swap(array, distance, high_distance=None):
    count = lax.axis_size("gx")
    high_distance = high_distance or distance
    pairs = [(i, i ^ (distance if i < count // 2 else high_distance)) for i in range(count)]
    return lax.ppermute(array, "gx", pairs)


def line_ends(mine, give):
    rows, width = mine.shape[1:]
    half = width // 2
    got = swap(give, 1)
    core_tie, part, give = call(
        core_kernel,
        [shape_of(8, rows, width), shape_of(7, rows, half), shape_of(7, rows, half)],
        [],
        mine,
        got,
    )
    got = swap(give, 3)
    chip_tie, block = call(
        chip_kernel, [shape_of(8, rows, half), shape_of(7, rows, half)], [], part, got
    )
    four = [shape_of(8, rows, half), shape_of(3, rows, half)]
    ends = [shape_of(4, rows, half)] * 2
    low_tie, low_rim = call(four_kernel, four, [], block, swap(block, 7, 1))
    from_low = swap(low_rim, 15)
    high_tie, high_rim = call(four_kernel, four, [], block, swap(block, 1, 7))
    from_high = swap(high_rim, 15)
    high_part, give = call(middle_kernel, ends, [], high_rim, from_low, high_tie, chip_tie)
    high_got = swap(give, 1, 3)
    low_part, give = call(middle_kernel, ends, [], low_rim, from_high, low_tie, chip_tie)
    low_got = swap(give, 3, 1)
    sides = (low_part, low_got, high_part, high_got)
    return call(spread_kernel, [shape_of(4, rows, width)] * 2, [], *sides, core_tie)


def lanes_of(is_mine, width):
    first = half_first() if is_mine else jnp.logical_not(half_first())
    return pl.ds(pl.multiple_of(jnp.where(first, 0, width), LANES), width)


def back_sweep(lanes, factor_ref, left_ref, down_ref, below, above, scale, out_ref):
    value = above
    for k in range(out_ref.shape[0] - 1, -1, -1):
        value = down_ref[k, :, lanes] + left_ref[k, :, lanes] * below + factor_ref[k, :, lanes] * value
        out_ref[k] = value * scale


def patch_sums(patch_count, total_rows, lanes, map_ref, adj_ref, new_ref):
    planes, rows, width = adj_ref.shape
    damping = damping_rows(rows, total_rows)
    patch_rows = PATCH_ROWS
    patch_lanes = patch_count // patch_rows
    row_ids = lax.broadcasted_iota(jnp.int32, (patch_rows, width), 0)
    lane_ids = lax.broadcasted_iota(jnp.int32, (patch_lanes, width), 0)
    total = jnp.zeros((3 * patch_rows, patch_lanes), F32)
    for k in range(planes):
        cells = jnp.sum(adj_ref[k] * new_ref[k] * damping, axis=0, keepdims=True)
        patches = map_ref[k : k + 1, lanes]
        first = cells.astype(jnp.bfloat16).astype(F32)
        rest = cells - first
        second = rest.astype(jnp.bfloat16).astype(F32)
        third = rest - second
        in_row = row_ids == patches // patch_lanes
        parts = jnp.concatenate(
            [jnp.where(in_row, part, 0.0) for part in (first, second, third)], axis=0
        ).astype(jnp.bfloat16)
        places = jnp.where(lane_ids == patches % patch_lanes, 1.0, 0.0).astype(jnp.bfloat16)
        total = total + lax.dot_general(
            parts, places, (((1,), (1,)), ((), ())), preferred_element_type=F32
        )
    return total[:patch_rows] + total[patch_rows : 2 * patch_rows] + total[2 * patch_rows :]


def own_half_kernel(
    patch_count, stiffness, total_rows, factor_ref, left_ref, adj_down_ref, down_ref, ends_ref, map_ref,
    adj_ref, new_ref, sums_ref,
):
    lanes = lanes_of(True, adj_ref.shape[2])
    sweep = (lanes, factor_ref, left_ref)
    back_sweep(*sweep, adj_down_ref, ends_ref[0], ends_ref[1], 1.0 / stiffness, adj_ref)
    back_sweep(*sweep, down_ref, ends_ref[2], ends_ref[3], 1.0 / stiffness, new_ref)
    sums_ref[...] = patch_sums(patch_count, total_rows, lanes, map_ref, adj_ref, new_ref)


def adjoint_kernel(
    stiffness, total_rows, factor_ref, left_ref, adj_down_ref, ends_ref, mine_ref,
    adj_ref, first_ref, second_ref,
):
    lanes = lanes_of(False, adj_ref.shape[2])
    back_sweep(
        lanes, factor_ref, left_ref, adj_down_ref, ends_ref[0], ends_ref[1], 1.0 / stiffness, adj_ref
    )
    for k in range(adj_ref.shape[0]):
        edges((first_ref, second_ref), k, joined(half_first(), mine_ref[k], adj_ref[k]))


def shares_kernel(
    patch_count, stiffness, total_rows, factor_ref, left_ref, down_ref, ends_ref, map_ref, adj_ref, mine_ref,
    new_ref, shares_ref,
):
    lanes = lanes_of(False, adj_ref.shape[2])
    back_sweep(
        lanes, factor_ref, left_ref, down_ref, ends_ref[2], ends_ref[3], 1.0 / stiffness, new_ref
    )
    sums = mine_ref[...] + patch_sums(patch_count, total_rows, lanes, map_ref, adj_ref, new_ref)
    rows_here = sums.shape[0]
    for i in range(shares_ref.shape[0] // rows_here):
        shares_ref[i * rows_here : (i + 1) * rows_here, :] = sums


def gradient_kernel(
    norm_factor, adj_ref, adj_got_ref, new_in_ref, new_got_ref, second_ref, first_ref, broken_ref,
    out_ref, new_ref, weight_ref,
):
    for k in range(adj_ref.shape[0]):
        adjoint = joined(half_first(), adj_ref[k], adj_got_ref[k])
        out_ref[k] = explicit(adjoint, *halo(first_ref, second_ref, k))
        new_ref[k] = joined(half_first(), new_in_ref[k], new_got_ref[k])
    weight_ref[...] = -(1 - broken_ref[...]).astype(F32) * norm_factor


def patch_kernel(shares_ref, weight_ref, out_ref):
    owned = weight_ref.shape[1]
    width = shares_ref.shape[1]
    total = jnp.sum(shares_ref[...], axis=0, keepdims=True)
    total = jnp.broadcast_to(jnp.concatenate([total] * (LANES // width), axis=1), (8, LANES))
    shift = lax.rem(LANES - owned * lax.axis_index("gy"), LANES)
    out_ref[...] = weight_ref[...] * pltpu.roll(total, shift, 1)[:1, :owned]


def call(kernel, outs, scratch, *operands):
    return pl.pallas_call(
        kernel,
        out_shape=outs,
        in_specs=[VMEM] * len(operands),
        out_specs=[VMEM] * len(outs),
        scratch_shapes=scratch,
        compiler_params=pltpu.CompilerParams(vmem_limit_bytes=32 * 1024 * 1024),
    )(*operands)


def local(velocity, cotangent, shape_coef, patch_map, broken):
    planes, rows, span = velocity.shape
    groups_x = lax.axis_size("gx")
    groups_y = lax.axis_size("gy")
    total_rows = rows * groups_y
    stiffness = 3.0 * planes * planes
    field = (planes, rows, span)
    plane = (planes, span)

    def with_sizes(kernel):
        return lambda *refs: kernel(stiffness, total_rows, *refs)

    velocity, first, second = call(
        edge_kernel, [shape_of(*field), shape_of(*plane), shape_of(*plane)], [], velocity
    )
    first, second = pair_swap(first, second)
    factor, adj_down, left, rims = call(
        with_sizes(matrix_kernel),
        [shape_of(*field)] * 3 + [shape_of(5, rows, span)],
        [],
        shape_coef,
        cotangent,
    )
    down, mine, give = call(
        velocity_kernel,
        [shape_of(*field)] + [shape_of(7, rows, span // 2)] * 2,
        [],
        velocity,
        second,
        first,
        factor,
        rims,
    )
    mine, give = line_ends(mine, give)
    got = swap(give, 1)
    owned = broken.shape[0]
    devices = groups_x * groups_y
    patch_count = owned * devices
    half = (planes, rows, span // 2)
    adj_mine, new_mine, sums = call(
        with_sizes(functools.partial(own_half_kernel, patch_count)),
        [shape_of(*half), shape_of(*half), shape_of(PATCH_ROWS, patch_count // PATCH_ROWS)],
        [],
        factor,
        left,
        adj_down,
        down,
        mine,
        patch_map,
    )
    adj_got, first, second = call(
        with_sizes(adjoint_kernel),
        [shape_of(*half), shape_of(*plane), shape_of(*plane)],
        [],
        factor,
        left,
        adj_down,
        got,
        adj_mine,
    )
    first, second = pair_swap(first, second)
    new_got, sums = call(
        with_sizes(functools.partial(shares_kernel, patch_count)),
        [shape_of(*half), shape_of(devices, patch_count // PATCH_ROWS)],
        [],
        factor,
        left,
        down,
        got,
        patch_map,
        adj_got,
        sums,
    )
    shares = lax.all_to_all(sums, ("gy", "gx"), 0, 0, tiled=True)
    norm_factor = 1.0 / math.sqrt(planes * groups_x * total_rows * span / (owned * devices))
    grad_velocity, new_velocity, weight = call(
        functools.partial(gradient_kernel, norm_factor),
        [shape_of(*field), shape_of(*field), shape_of(1, owned)],
        [],
        adj_mine,
        adj_got,
        new_mine,
        new_got,
        second,
        first,
        broken.reshape(1, owned),
    )
    (patch_sens,) = call(patch_kernel, [shape_of(1, owned)], [], shares, weight)
    return (new_velocity, grad_velocity, patch_sens.reshape(owned))


def solution(mesh):
    return jax.shard_map(
        local,
        mesh=mesh,
        in_specs=(
            P("gx", "gy", None),
            P("gx", "gy", None),
            P("gx", None),
            P("gx", None),
            P(("gx", "gy")),
        ),
        out_specs=(P("gx", "gy", None), P("gx", "gy", None), P(("gx", "gy"))),
        check_vma=False,
    )
```

```python
import functools
import math

import jax
import jax.numpy as jnp
from jax import lax
from jax.experimental import pallas as pl
from jax.experimental.pallas import tpu as pltpu
from jax.sharding import PartitionSpec as P

wall_coef = 0.2
span_coef = 0.15
wall_decay = 8.0
VMEM = pl.BlockSpec(memory_space=pltpu.VMEM)
F32 = jnp.float32
LANES = 128
PATCH_ROWS = 16


def shape_of(*dims):
    return jax.ShapeDtypeStruct(dims, F32)


def explicit(field, below, above):
    rows, span = field.shape
    row_ids = lax.broadcasted_iota(jnp.int32, (rows, span), 0)
    lower = jnp.where(row_ids == 0, below, pltpu.roll(field, 1, 0))
    upper = jnp.where(row_ids == rows - 1, above, pltpu.roll(field, rows - 1, 0))
    wall_term = upper + lower - 2.0 * field
    span_term = pltpu.roll(field, 1, 1) + pltpu.roll(field, span - 1, 1) - 2.0 * field
    return field + wall_coef * wall_term + span_coef * span_term


def edges(refs, k, field):
    first_ref, second_ref = refs
    rows = field.shape[0]
    even = lax.axis_index("gy") % 2 == 0
    low, high = field[:1], field[rows - 1 :]
    first_ref[k : k + 1, :] = jnp.where(even, high, low)
    second_ref[k : k + 1, :] = jnp.where(even, low, high)


def halo(first_ref, second_ref, k):
    position = lax.axis_index("gy")
    even = position % 2 == 0
    inner = (position > 0) & (position < lax.axis_size("gy") - 1)
    first = first_ref[k : k + 1, :]
    second = jnp.where(inner, second_ref[k : k + 1, :], 0.0)
    return jnp.where(even, second, first), jnp.where(even, first, second)


def near_swap(edge):
    return lax.ppermute(edge, "gy", [(i, i ^ 1) for i in range(lax.axis_size("gy"))])


def far_swap(edge):
    count_x, count = lax.axis_size("gx"), lax.axis_size("gy")
    pairs = []
    for i in range(count_x):
        for j in range(count):
            target = j + 1 if j % 2 else j - 1
            inside = 0 <= target < count
            pairs.append((i * count + j, i * count + target if inside else (i ^ 1) * count + j))
    return lax.ppermute(edge, ("gx", "gy"), pairs)


def pair_swap(first, second):
    return near_swap(first), far_swap(second)


def edge_kernel(velocity_ref, held_ref, first_ref, second_ref):
    for k in range(velocity_ref.shape[0]):
        held_ref[k] = velocity_ref[k]
        edges((first_ref, second_ref), k, velocity_ref[k])


def damping_rows(rows, total_rows):
    first = lax.axis_index("gy") * rows
    heights = (first + lax.broadcasted_iota(jnp.int32, (rows, 1), 0)).astype(F32)
    return jnp.exp(-wall_decay * heights / total_rows)


def matrix_kernel(stiffness, total_rows, coef_ref, target_ref, factor_ref, adj_down_ref, left_ref, rims_ref):
    planes, rows, span = target_ref.shape
    damping = damping_rows(rows, total_rows)
    factor = jnp.zeros((rows, span), F32)
    reduced = jnp.zeros((rows, span), F32)
    left = jnp.ones((rows, span), F32)
    for k in range(planes):
        diagonal = 1.0 + 2.0 * stiffness + coef_ref[k : k + 1, :] * damping
        factor = stiffness / (diagonal - stiffness * factor)
        reduced = (target_ref[k] + reduced) * factor
        left = left * factor
        factor_ref[k] = factor
        adj_down_ref[k] = reduced
        left_ref[k] = left
    value, right = reduced, factor
    rims_ref[1] = left
    rims_ref[2] = factor
    rims_ref[4] = reduced
    for k in range(planes - 2, -1, -1):
        factor = factor_ref[k]
        value = adj_down_ref[k] + factor * value
        left = left_ref[k] + factor * left
    rims_ref[0] = left
    rims_ref[3] = value


def velocity_kernel(velocity_ref, second_ref, first_ref, factor_ref, rims_ref, down_ref, mine_ref, give_ref):
    planes, rows, span = velocity_ref.shape
    reduced = jnp.zeros((rows, span), F32)
    for k in range(planes):
        forcing = explicit(velocity_ref[k], *halo(first_ref, second_ref, k))
        reduced = (forcing + reduced) * factor_ref[k]
        down_ref[k] = reduced
    value = reduced
    for k in range(planes - 2, -1, -1):
        value = down_ref[k] + factor_ref[k] * value
    pieces = [rims_ref[i] for i in range(5)] + [value, reduced]
    split(half_first(), pieces, mine_ref, give_ref)


def place():
    position = lax.axis_index("gx")
    return position % 2, position // 2


def split(first, pieces, mine_ref, give_ref):
    width = mine_ref.shape[2]
    for i, piece in enumerate(pieces):
        low, high = piece[:, :width], piece[:, width:]
        mine_ref[i] = jnp.where(first, low, high)
        give_ref[i] = jnp.where(first, high, low)


def joined(first, mine, other):
    return jnp.concatenate([jnp.where(first, mine, other), jnp.where(first, other, mine)], axis=1)


def merged(is_left, mine_ref, other_ref, tie_ref):
    left, right = [], []
    for i in range(7):
        mine, other = mine_ref[i], other_ref[i]
        left.append(jnp.where(is_left, mine, other))
        right.append(jnp.where(is_left, other, mine))
    top_l, cross_l, low_l, *sides_l = left
    top_r, cross_r, low_r, *sides_r = right
    inverse = 1.0 / (1.0 - low_l * top_r)
    to_left, to_right = cross_l * inverse, cross_r * inverse
    through_top, through_low = top_r * to_left, low_l * to_right
    tie_ref[0], tie_ref[1], tie_ref[2], tie_ref[3] = to_left, through_low, through_top, to_right
    block = [top_l + cross_l * through_top, cross_l * to_right, low_r + cross_r * through_low]
    for side in range(2):
        tops_l, lows_l = sides_l[2 * side], sides_l[2 * side + 1]
        tops_r, lows_r = sides_r[2 * side], sides_r[2 * side + 1]
        low = (lows_l + low_l * tops_r) * inverse
        top = (tops_r + top_r * lows_l) * inverse
        tie_ref[4 + 2 * side], tie_ref[5 + 2 * side] = low, top
        block += [tops_l + cross_l * top, lows_r + cross_r * low]
    return block


def untied(tie_ref, outer):
    inner = []
    for side in range(2):
        below, above = outer[2 * side], outer[2 * side + 1]
        low = tie_ref[4 + 2 * side] + tie_ref[0] * below + tie_ref[1] * above
        top = tie_ref[5 + 2 * side] + tie_ref[2] * below + tie_ref[3] * above
        inner.append((low, top))
    (low_a, top_a), (low_v, top_v) = inner
    return (
        [outer[0], top_a, outer[2], top_v],
        [low_a, outer[1], low_v, outer[3]],
    )


def chosen(is_left, pair):
    return [jnp.where(is_left, x, y) for x, y in zip(*pair)]


def half_first():
    core, chip = place()
    return (core + chip) % 2 == 0


def quarter_first():
    _, chip = place()
    return (chip + chip // 2) % 2 == 0


def core_kernel(mine_ref, got_ref, tie_ref, keep_ref, give_ref):
    core, _ = place()
    split(quarter_first(), merged(core == 0, mine_ref, got_ref, tie_ref), keep_ref, give_ref)


def chip_kernel(mine_ref, got_ref, tie_ref, block_ref):
    _, chip = place()
    for i, value in enumerate(merged(chip % 2 == 0, mine_ref, got_ref, tie_ref)):
        block_ref[i] = value


def four_kernel(mine_ref, got_ref, tie_ref, rim_ref):
    _, chip = place()
    top, _, low, *sides = merged(chip // 2 % 2 == 0, mine_ref, got_ref, tie_ref)
    is_left = chip < 4
    rim_ref[0] = jnp.where(is_left, low, top)
    rim_ref[1] = jnp.where(is_left, sides[1], sides[0])
    rim_ref[2] = jnp.where(is_left, sides[3], sides[2])


def middle_kernel(rim_ref, got_ref, four_tie_ref, chip_tie_ref, mine_ref, give_ref):
    _, chip = place()
    is_left = chip < 4
    rim, got = rim_ref[0], got_ref[0]
    inverse = 1.0 / (1.0 - rim * got)
    outer = []
    for side in (1, 2):
        across = (got_ref[side] + got * rim_ref[side]) * inverse
        outer += [jnp.where(is_left, 0.0, across), jnp.where(is_left, across, 0.0)]
    outer = chosen(chip // 2 % 2 == 0, untied(four_tie_ref, outer))
    left, right = untied(chip_tie_ref, outer)
    for i in range(4):
        mine_ref[i] = jnp.where(chip % 2 == 0, left[i], right[i])
        give_ref[i] = jnp.where(chip % 2 == 0, right[i], left[i])


def spread_kernel(low_part_ref, low_got_ref, high_part_ref, high_got_ref, tie_ref, mine_ref, give_ref):
    core, chip = place()
    first = quarter_first()
    is_low = chip < 4
    outer = [
        joined(
            first,
            jnp.where(is_low, low_part_ref[i], high_part_ref[i]),
            jnp.where(is_low, low_got_ref[i], high_got_ref[i]),
        )
        for i in range(4)
    ]
    left, right = untied(tie_ref, outer)
    for i in range(4):
        mine_ref[i] = jnp.where(core == 0, left[i], right[i])
        give_ref[i] = jnp.where(core == 0, right[i], left[i])


def swap(array, distance, high_distance=None):
    count = lax.axis_size("gx")
    high_distance = high_distance or distance
    pairs = [(i, i ^ (distance if i < count // 2 else high_distance)) for i in range(count)]
    return lax.ppermute(array, "gx", pairs)


def line_ends(mine, give):
    rows, width = mine.shape[1:]
    half = width // 2
    got = swap(give, 1)
    core_tie, part, give = call(
        core_kernel,
        [shape_of(8, rows, width), shape_of(7, rows, half), shape_of(7, rows, half)],
        [],
        mine,
        got,
    )
    got = swap(give, 3)
    chip_tie, block = call(
        chip_kernel, [shape_of(8, rows, half), shape_of(7, rows, half)], [], part, got
    )
    four = [shape_of(8, rows, half), shape_of(3, rows, half)]
    ends = [shape_of(4, rows, half)] * 2
    low_tie, low_rim = call(four_kernel, four, [], block, swap(block, 7, 1))
    from_low = swap(low_rim, 15)
    high_tie, high_rim = call(four_kernel, four, [], block, swap(block, 1, 7))
    from_high = swap(high_rim, 15)
    high_part, give = call(middle_kernel, ends, [], high_rim, from_low, high_tie, chip_tie)
    high_got = swap(give, 1, 3)
    low_part, give = call(middle_kernel, ends, [], low_rim, from_high, low_tie, chip_tie)
    low_got = swap(give, 3, 1)
    sides = (low_part, low_got, high_part, high_got)
    return call(spread_kernel, [shape_of(4, rows, width)] * 2, [], *sides, core_tie)


def lanes_of(is_mine, width):
    first = half_first() if is_mine else jnp.logical_not(half_first())
    return pl.ds(pl.multiple_of(jnp.where(first, 0, width), LANES), width)


def back_sweep(lanes, factor_ref, left_ref, down_ref, below, above, scale, out_ref):
    value = above
    for k in range(out_ref.shape[0] - 1, -1, -1):
        value = down_ref[k, :, lanes] + left_ref[k, :, lanes] * below + factor_ref[k, :, lanes] * value
        out_ref[k] = value * scale


def patch_sums(patch_count, total_rows, lanes, map_ref, adj_ref, new_ref):
    planes, rows, width = adj_ref.shape
    damping = damping_rows(rows, total_rows)
    patch_rows = PATCH_ROWS
    patch_lanes = patch_count // patch_rows
    row_ids = lax.broadcasted_iota(jnp.int32, (patch_rows, width), 0)
    lane_ids = lax.broadcasted_iota(jnp.int32, (patch_lanes, width), 0)
    total = jnp.zeros((3 * patch_rows, patch_lanes), F32)
    for k in range(planes):
        cells = jnp.sum(adj_ref[k] * new_ref[k] * damping, axis=0, keepdims=True)
        patches = map_ref[k : k + 1, lanes]
        first = cells.astype(jnp.bfloat16).astype(F32)
        rest = cells - first
        second = rest.astype(jnp.bfloat16).astype(F32)
        third = rest - second
        in_row = row_ids == patches // patch_lanes
        parts = jnp.concatenate(
            [jnp.where(in_row, part, 0.0) for part in (first, second, third)], axis=0
        ).astype(jnp.bfloat16)
        places = jnp.where(lane_ids == patches % patch_lanes, 1.0, 0.0).astype(jnp.bfloat16)
        total = total + lax.dot_general(
            parts, places, (((1,), (1,)), ((), ())), preferred_element_type=F32
        )
    return total[:patch_rows] + total[patch_rows : 2 * patch_rows] + total[2 * patch_rows :]


def own_half_kernel(
    patch_count, stiffness, total_rows, factor_ref, left_ref, adj_down_ref, down_ref, ends_ref, map_ref,
    adj_ref, new_ref, sums_ref,
):
    lanes = lanes_of(True, adj_ref.shape[2])
    sweep = (lanes, factor_ref, left_ref)
    back_sweep(*sweep, adj_down_ref, ends_ref[0], ends_ref[1], 1.0 / stiffness, adj_ref)
    back_sweep(*sweep, down_ref, ends_ref[2], ends_ref[3], 1.0 / stiffness, new_ref)
    sums_ref[...] = patch_sums(patch_count, total_rows, lanes, map_ref, adj_ref, new_ref)


def adjoint_edges_kernel(mine_ref, got_ref, first_ref, second_ref):
    for k in range(mine_ref.shape[0]):
        edges((first_ref, second_ref), k, joined(half_first(), mine_ref[k], got_ref[k]))


def shares_kernel(
    patch_count, stiffness, total_rows, factor_ref, left_ref, adj_down_ref, down_ref, ends_ref, map_ref, mine_ref,
    adj_ref, new_ref, shares_ref,
):
    lanes = lanes_of(False, adj_ref.shape[2])
    sweep = (lanes, factor_ref, left_ref)
    back_sweep(*sweep, adj_down_ref, ends_ref[0], ends_ref[1], 1.0 / stiffness, adj_ref)
    back_sweep(*sweep, down_ref, ends_ref[2], ends_ref[3], 1.0 / stiffness, new_ref)
    sums = mine_ref[...] + patch_sums(patch_count, total_rows, lanes, map_ref, adj_ref, new_ref)
    rows_here = sums.shape[0]
    for i in range(shares_ref.shape[0] // rows_here):
        shares_ref[i * rows_here : (i + 1) * rows_here, :] = sums


def gradient_kernel(
    norm_factor, adj_ref, adj_got_ref, new_in_ref, new_got_ref, second_ref, first_ref, broken_ref,
    out_ref, new_ref, weight_ref,
):
    for k in range(adj_ref.shape[0]):
        adjoint = joined(half_first(), adj_ref[k], adj_got_ref[k])
        out_ref[k] = explicit(adjoint, *halo(first_ref, second_ref, k))
        new_ref[k] = joined(half_first(), new_in_ref[k], new_got_ref[k])
    weight_ref[...] = -(1 - broken_ref[...]).astype(F32) * norm_factor


def patch_kernel(shares_ref, weight_ref, out_ref):
    owned = weight_ref.shape[1]
    width = shares_ref.shape[1]
    total = jnp.sum(shares_ref[...], axis=0, keepdims=True)
    total = jnp.broadcast_to(jnp.concatenate([total] * (LANES // width), axis=1), (8, LANES))
    shift = lax.rem(LANES - owned * lax.axis_index("gy"), LANES)
    out_ref[...] = weight_ref[...] * pltpu.roll(total, shift, 1)[:1, :owned]


def call(kernel, outs, scratch, *operands):
    return pl.pallas_call(
        kernel,
        out_shape=outs,
        in_specs=[VMEM] * len(operands),
        out_specs=[VMEM] * len(outs),
        scratch_shapes=scratch,
        compiler_params=pltpu.CompilerParams(vmem_limit_bytes=32 * 1024 * 1024),
    )(*operands)


def local(velocity, cotangent, shape_coef, patch_map, broken):
    planes, rows, span = velocity.shape
    groups_x = lax.axis_size("gx")
    groups_y = lax.axis_size("gy")
    total_rows = rows * groups_y
    stiffness = 3.0 * planes * planes
    field = (planes, rows, span)
    plane = (planes, span)

    def with_sizes(kernel):
        return lambda *refs: kernel(stiffness, total_rows, *refs)

    velocity, first, second = call(
        edge_kernel, [shape_of(*field), shape_of(*plane), shape_of(*plane)], [], velocity
    )
    first, second = pair_swap(first, second)
    factor, adj_down, left, rims = call(
        with_sizes(matrix_kernel),
        [shape_of(*field)] * 3 + [shape_of(5, rows, span)],
        [],
        shape_coef,
        cotangent,
    )
    down, mine, give = call(
        velocity_kernel,
        [shape_of(*field)] + [shape_of(7, rows, span // 2)] * 2,
        [],
        velocity,
        second,
        first,
        factor,
        rims,
    )
    mine, give = line_ends(mine, give)
    got = swap(give, 1)
    owned = broken.shape[0]
    devices = groups_x * groups_y
    patch_count = owned * devices
    half = (planes, rows, span // 2)
    adj_mine, new_mine, sums = call(
        with_sizes(functools.partial(own_half_kernel, patch_count)),
        [shape_of(*half), shape_of(*half), shape_of(PATCH_ROWS, patch_count // PATCH_ROWS)],
        [],
        factor,
        left,
        adj_down,
        down,
        mine,
        patch_map,
    )
    adj_got, new_got, sums = call(
        with_sizes(functools.partial(shares_kernel, patch_count)),
        [shape_of(*half), shape_of(*half), shape_of(devices, patch_count // PATCH_ROWS)],
        [],
        factor,
        left,
        adj_down,
        down,
        got,
        patch_map,
        sums,
    )
    first, second = call(
        adjoint_edges_kernel, [shape_of(*plane), shape_of(*plane)], [], adj_mine, adj_got
    )
    first, second = pair_swap(first, second)
    shares = lax.all_to_all(sums, ("gy", "gx"), 0, 0, tiled=True)
    norm_factor = 1.0 / math.sqrt(planes * groups_x * total_rows * span / (owned * devices))
    grad_velocity, new_velocity, weight = call(
        functools.partial(gradient_kernel, norm_factor),
        [shape_of(*field), shape_of(*field), shape_of(1, owned)],
        [],
        adj_mine,
        adj_got,
        new_mine,
        new_got,
        second,
        first,
        broken.reshape(1, owned),
    )
    (patch_sens,) = call(patch_kernel, [shape_of(1, owned)], [], shares, weight)
    return (new_velocity, grad_velocity, patch_sens.reshape(owned))


def solution(mesh):
    return jax.shard_map(
        local,
        mesh=mesh,
        in_specs=(
            P("gx", "gy", None),
            P("gx", "gy", None),
            P("gx", None),
            P("gx", None),
            P(("gx", "gy")),
        ),
        out_specs=(P("gx", "gy", None), P("gx", "gy", None), P(("gx", "gy"))),
        check_vma=False,
    )
```

```python
import functools
import math

import jax
import jax.numpy as jnp
from jax import lax
from jax.experimental import pallas as pl
from jax.experimental.pallas import tpu as pltpu
from jax.sharding import PartitionSpec as P

wall_coef = 0.2
span_coef = 0.15
wall_decay = 8.0
VMEM = pl.BlockSpec(memory_space=pltpu.VMEM)
F32 = jnp.float32
LANES = 128
PATCH_ROWS = 16


def shape_of(*dims):
    return jax.ShapeDtypeStruct(dims, F32)


def explicit(field, below, above):
    rows, span = field.shape
    row_ids = lax.broadcasted_iota(jnp.int32, (rows, span), 0)
    lower = jnp.where(row_ids == 0, below, pltpu.roll(field, 1, 0))
    upper = jnp.where(row_ids == rows - 1, above, pltpu.roll(field, rows - 1, 0))
    wall_term = upper + lower - 2.0 * field
    span_term = pltpu.roll(field, 1, 1) + pltpu.roll(field, span - 1, 1) - 2.0 * field
    return field + wall_coef * wall_term + span_coef * span_term


def edges(refs, k, field):
    first_ref, second_ref = refs
    rows = field.shape[0]
    even = lax.axis_index("gy") % 2 == 0
    low, high = field[:1], field[rows - 1 :]
    first_ref[k : k + 1, :] = jnp.where(even, high, low)
    second_ref[k : k + 1, :] = jnp.where(even, low, high)


def halo(first_ref, second_ref, k):
    position = lax.axis_index("gy")
    even = position % 2 == 0
    inner = (position > 0) & (position < lax.axis_size("gy") - 1)
    first = first_ref[k : k + 1, :]
    second = jnp.where(inner, second_ref[k : k + 1, :], 0.0)
    return jnp.where(even, second, first), jnp.where(even, first, second)


def near_swap(edge):
    return lax.ppermute(edge, "gy", [(i, i ^ 1) for i in range(lax.axis_size("gy"))])


def far_swap(edge):
    count_x, count = lax.axis_size("gx"), lax.axis_size("gy")
    pairs = []
    for i in range(count_x):
        for j in range(count):
            target = j + 1 if j % 2 else j - 1
            inside = 0 <= target < count
            pairs.append((i * count + j, i * count + target if inside else (i ^ 1) * count + j))
    return lax.ppermute(edge, ("gx", "gy"), pairs)


def pair_swap(first, second):
    return near_swap(first), far_swap(second)


def edge_kernel(velocity_ref, held_ref, first_ref, second_ref):
    for k in range(velocity_ref.shape[0]):
        held_ref[k] = velocity_ref[k]
        edges((first_ref, second_ref), k, velocity_ref[k])


def damping_rows(rows, total_rows):
    first = lax.axis_index("gy") * rows
    heights = (first + lax.broadcasted_iota(jnp.int32, (rows, 1), 0)).astype(F32)
    return jnp.exp(-wall_decay * heights / total_rows)


def matrix_kernel(
    stiffness, total_rows, coef_ref, target_ref, velocity_ref, map_ref,
    factor_ref, adj_down_ref, left_ref, rims_ref, base_ref, map_out_ref,
):
    map_out_ref[...] = map_ref[...]
    for k in range(velocity_ref.shape[0]):
        base_ref[k] = explicit(velocity_ref[k], 0.0, 0.0)
    planes, rows, span = target_ref.shape
    damping = damping_rows(rows, total_rows)
    factor = jnp.zeros((rows, span), F32)
    reduced = jnp.zeros((rows, span), F32)
    left = jnp.ones((rows, span), F32)
    for k in range(planes):
        diagonal = 1.0 + 2.0 * stiffness + coef_ref[k : k + 1, :] * damping
        factor = stiffness / (diagonal - stiffness * factor)
        reduced = (target_ref[k] + reduced) * factor
        left = left * factor
        factor_ref[k] = factor
        adj_down_ref[k] = reduced
        left_ref[k] = left
    value, right = reduced, factor
    rims_ref[1] = left
    rims_ref[2] = factor
    rims_ref[4] = reduced
    for k in range(planes - 2, -1, -1):
        factor = factor_ref[k]
        value = adj_down_ref[k] + factor * value
        left = left_ref[k] + factor * left
    rims_ref[0] = left
    rims_ref[3] = value


def velocity_kernel(base_ref, second_ref, first_ref, factor_ref, rims_ref, down_ref, mine_ref, give_ref):
    planes, rows, span = base_ref.shape
    row_ids = lax.broadcasted_iota(jnp.int32, (rows, span), 0)
    reduced = jnp.zeros((rows, span), F32)
    for k in range(planes):
        below, above = halo(first_ref, second_ref, k)
        outside = jnp.where(row_ids == 0, below, jnp.where(row_ids == rows - 1, above, 0.0))
        forcing = base_ref[k] + wall_coef * outside
        reduced = (forcing + reduced) * factor_ref[k]
        down_ref[k] = reduced
    value = reduced
    for k in range(planes - 2, -1, -1):
        value = down_ref[k] + factor_ref[k] * value
    pieces = [rims_ref[i] for i in range(5)] + [value, reduced]
    split(half_first(), pieces, mine_ref, give_ref)


def place():
    position = lax.axis_index("gx")
    return position % 2, position // 2


def split(first, pieces, mine_ref, give_ref):
    width = mine_ref.shape[2]
    for i, piece in enumerate(pieces):
        low, high = piece[:, :width], piece[:, width:]
        mine_ref[i] = jnp.where(first, low, high)
        give_ref[i] = jnp.where(first, high, low)


def joined(first, mine, other):
    return jnp.concatenate([jnp.where(first, mine, other), jnp.where(first, other, mine)], axis=1)


def merged(is_left, mine_ref, other_ref, tie_ref):
    left, right = [], []
    for i in range(7):
        mine, other = mine_ref[i], other_ref[i]
        left.append(jnp.where(is_left, mine, other))
        right.append(jnp.where(is_left, other, mine))
    top_l, cross_l, low_l, *sides_l = left
    top_r, cross_r, low_r, *sides_r = right
    inverse = 1.0 / (1.0 - low_l * top_r)
    to_left, to_right = cross_l * inverse, cross_r * inverse
    through_top, through_low = top_r * to_left, low_l * to_right
    tie_ref[0], tie_ref[1], tie_ref[2], tie_ref[3] = to_left, through_low, through_top, to_right
    block = [top_l + cross_l * through_top, cross_l * to_right, low_r + cross_r * through_low]
    for side in range(2):
        tops_l, lows_l = sides_l[2 * side], sides_l[2 * side + 1]
        tops_r, lows_r = sides_r[2 * side], sides_r[2 * side + 1]
        low = (lows_l + low_l * tops_r) * inverse
        top = (tops_r + top_r * lows_l) * inverse
        tie_ref[4 + 2 * side], tie_ref[5 + 2 * side] = low, top
        block += [tops_l + cross_l * top, lows_r + cross_r * low]
    return block


def untied(tie_ref, outer):
    inner = []
    for side in range(2):
        below, above = outer[2 * side], outer[2 * side + 1]
        low = tie_ref[4 + 2 * side] + tie_ref[0] * below + tie_ref[1] * above
        top = tie_ref[5 + 2 * side] + tie_ref[2] * below + tie_ref[3] * above
        inner.append((low, top))
    (low_a, top_a), (low_v, top_v) = inner
    return (
        [outer[0], top_a, outer[2], top_v],
        [low_a, outer[1], low_v, outer[3]],
    )


def chosen(is_left, pair):
    return [jnp.where(is_left, x, y) for x, y in zip(*pair)]


def half_first():
    core, chip = place()
    return (core + chip) % 2 == 0


def quarter_first():
    _, chip = place()
    return (chip + chip // 2) % 2 == 0


def core_kernel(mine_ref, got_ref, tie_ref, keep_ref, give_ref):
    core, _ = place()
    split(quarter_first(), merged(core == 0, mine_ref, got_ref, tie_ref), keep_ref, give_ref)


def chip_kernel(mine_ref, got_ref, tie_ref, block_ref):
    _, chip = place()
    for i, value in enumerate(merged(chip % 2 == 0, mine_ref, got_ref, tie_ref)):
        block_ref[i] = value


def four_kernel(mine_ref, got_ref, tie_ref, rim_ref):
    _, chip = place()
    top, _, low, *sides = merged(chip // 2 % 2 == 0, mine_ref, got_ref, tie_ref)
    is_left = chip < 4
    rim_ref[0] = jnp.where(is_left, low, top)
    rim_ref[1] = jnp.where(is_left, sides[1], sides[0])
    rim_ref[2] = jnp.where(is_left, sides[3], sides[2])


def middle_kernel(rim_ref, got_ref, four_tie_ref, chip_tie_ref, mine_ref, give_ref):
    _, chip = place()
    is_left = chip < 4
    rim, got = rim_ref[0], got_ref[0]
    inverse = 1.0 / (1.0 - rim * got)
    outer = []
    for side in (1, 2):
        across = (got_ref[side] + got * rim_ref[side]) * inverse
        outer += [jnp.where(is_left, 0.0, across), jnp.where(is_left, across, 0.0)]
    outer = chosen(chip // 2 % 2 == 0, untied(four_tie_ref, outer))
    left, right = untied(chip_tie_ref, outer)
    for i in range(4):
        mine_ref[i] = jnp.where(chip % 2 == 0, left[i], right[i])
        give_ref[i] = jnp.where(chip % 2 == 0, right[i], left[i])


def spread_kernel(low_part_ref, low_got_ref, high_part_ref, high_got_ref, tie_ref, mine_ref, give_ref):
    core, chip = place()
    first = quarter_first()
    is_low = chip < 4
    outer = [
        joined(
            first,
            jnp.where(is_low, low_part_ref[i], high_part_ref[i]),
            jnp.where(is_low, low_got_ref[i], high_got_ref[i]),
        )
        for i in range(4)
    ]
    left, right = untied(tie_ref, outer)
    for i in range(4):
        mine_ref[i] = jnp.where(core == 0, left[i], right[i])
        give_ref[i] = jnp.where(core == 0, right[i], left[i])


def swap(array, distance, high_distance=None):
    count = lax.axis_size("gx")
    high_distance = high_distance or distance
    pairs = [(i, i ^ (distance if i < count // 2 else high_distance)) for i in range(count)]
    return lax.ppermute(array, "gx", pairs)


def line_ends(mine, give):
    rows, width = mine.shape[1:]
    half = width // 2
    got = swap(give, 1)
    core_tie, part, give = call(
        core_kernel,
        [shape_of(8, rows, width), shape_of(7, rows, half), shape_of(7, rows, half)],
        [],
        mine,
        got,
    )
    got = swap(give, 3)
    chip_tie, block = call(
        chip_kernel, [shape_of(8, rows, half), shape_of(7, rows, half)], [], part, got
    )
    four = [shape_of(8, rows, half), shape_of(3, rows, half)]
    ends = [shape_of(4, rows, half)] * 2
    low_tie, low_rim = call(four_kernel, four, [], block, swap(block, 7, 1))
    from_low = swap(low_rim, 15)
    high_tie, high_rim = call(four_kernel, four, [], block, swap(block, 1, 7))
    from_high = swap(high_rim, 15)
    high_part, give = call(middle_kernel, ends, [], high_rim, from_low, high_tie, chip_tie)
    high_got = swap(give, 1, 3)
    low_part, give = call(middle_kernel, ends, [], low_rim, from_high, low_tie, chip_tie)
    low_got = swap(give, 3, 1)
    sides = (low_part, low_got, high_part, high_got)
    return call(spread_kernel, [shape_of(4, rows, width)] * 2, [], *sides, core_tie)


def lanes_of(is_mine, width):
    first = half_first() if is_mine else jnp.logical_not(half_first())
    return pl.ds(pl.multiple_of(jnp.where(first, 0, width), LANES), width)


def back_sweep(lanes, factor_ref, left_ref, down_ref, below, above, scale, out_ref):
    value = above
    for k in range(out_ref.shape[0] - 1, -1, -1):
        value = down_ref[k, :, lanes] + left_ref[k, :, lanes] * below + factor_ref[k, :, lanes] * value
        out_ref[k] = value * scale


def patch_sums(patch_count, total_rows, lanes, map_ref, adj_ref, new_ref):
    planes, rows, width = adj_ref.shape
    damping = damping_rows(rows, total_rows)
    patch_rows = PATCH_ROWS
    patch_lanes = patch_count // patch_rows
    row_ids = lax.broadcasted_iota(jnp.int32, (patch_rows, width), 0)
    lane_ids = lax.broadcasted_iota(jnp.int32, (patch_lanes, width), 0)
    total = jnp.zeros((3 * patch_rows, patch_lanes), F32)
    for k in range(planes):
        cells = jnp.sum(adj_ref[k] * new_ref[k] * damping, axis=0, keepdims=True)
        patches = map_ref[k : k + 1, lanes]
        first = cells.astype(jnp.bfloat16).astype(F32)
        rest = cells - first
        second = rest.astype(jnp.bfloat16).astype(F32)
        third = rest - second
        in_row = row_ids == patches // patch_lanes
        parts = jnp.concatenate(
            [jnp.where(in_row, part, 0.0) for part in (first, second, third)], axis=0
        ).astype(jnp.bfloat16)
        places = jnp.where(lane_ids == patches % patch_lanes, 1.0, 0.0).astype(jnp.bfloat16)
        total = total + lax.dot_general(
            parts, places, (((1,), (1,)), ((), ())), preferred_element_type=F32
        )
    return total[:patch_rows] + total[patch_rows : 2 * patch_rows] + total[2 * patch_rows :]


def own_half_kernel(
    patch_count, stiffness, total_rows, factor_ref, left_ref, adj_down_ref, down_ref, ends_ref, map_ref,
    adj_ref, new_ref, sums_ref,
):
    lanes = lanes_of(True, adj_ref.shape[2])
    sweep = (lanes, factor_ref, left_ref)
    back_sweep(*sweep, adj_down_ref, ends_ref[0], ends_ref[1], 1.0 / stiffness, adj_ref)
    back_sweep(*sweep, down_ref, ends_ref[2], ends_ref[3], 1.0 / stiffness, new_ref)
    sums_ref[...] = patch_sums(patch_count, total_rows, lanes, map_ref, adj_ref, new_ref)


def adjoint_edges_kernel(mine_ref, got_ref, first_ref, second_ref):
    for k in range(mine_ref.shape[0]):
        edges((first_ref, second_ref), k, joined(half_first(), mine_ref[k], got_ref[k]))


def shares_kernel(
    patch_count, stiffness, total_rows, factor_ref, left_ref, adj_down_ref, down_ref, ends_ref, map_ref, mine_ref,
    adj_ref, new_ref, shares_ref,
):
    lanes = lanes_of(False, adj_ref.shape[2])
    sweep = (lanes, factor_ref, left_ref)
    back_sweep(*sweep, adj_down_ref, ends_ref[0], ends_ref[1], 1.0 / stiffness, adj_ref)
    back_sweep(*sweep, down_ref, ends_ref[2], ends_ref[3], 1.0 / stiffness, new_ref)
    sums = mine_ref[...] + patch_sums(patch_count, total_rows, lanes, map_ref, adj_ref, new_ref)
    rows_here = sums.shape[0]
    for i in range(shares_ref.shape[0] // rows_here):
        shares_ref[i * rows_here : (i + 1) * rows_here, :] = sums


def gradient_kernel(
    norm_factor, adj_ref, adj_got_ref, new_in_ref, new_got_ref, second_ref, first_ref, broken_ref,
    out_ref, new_ref, weight_ref,
):
    for k in range(adj_ref.shape[0]):
        adjoint = joined(half_first(), adj_ref[k], adj_got_ref[k])
        out_ref[k] = explicit(adjoint, *halo(first_ref, second_ref, k))
        new_ref[k] = joined(half_first(), new_in_ref[k], new_got_ref[k])
    weight_ref[...] = -(1 - broken_ref[...]).astype(F32) * norm_factor


def patch_kernel(shares_ref, weight_ref, out_ref):
    owned = weight_ref.shape[1]
    width = shares_ref.shape[1]
    total = jnp.sum(shares_ref[...], axis=0, keepdims=True)
    total = jnp.broadcast_to(jnp.concatenate([total] * (LANES // width), axis=1), (8, LANES))
    shift = lax.rem(LANES - owned * lax.axis_index("gy"), LANES)
    out_ref[...] = weight_ref[...] * pltpu.roll(total, shift, 1)[:1, :owned]


def call(kernel, outs, scratch, *operands):
    return pl.pallas_call(
        kernel,
        out_shape=outs,
        in_specs=[VMEM] * len(operands),
        out_specs=[VMEM] * len(outs),
        scratch_shapes=scratch,
        compiler_params=pltpu.CompilerParams(vmem_limit_bytes=32 * 1024 * 1024),
    )(*operands)


def local(velocity, cotangent, shape_coef, patch_map, broken):
    planes, rows, span = velocity.shape
    groups_x = lax.axis_size("gx")
    groups_y = lax.axis_size("gy")
    total_rows = rows * groups_y
    stiffness = 3.0 * planes * planes
    field = (planes, rows, span)
    plane = (planes, span)

    def with_sizes(kernel):
        return lambda *refs: kernel(stiffness, total_rows, *refs)

    velocity, first, second = call(
        edge_kernel, [shape_of(*field), shape_of(*plane), shape_of(*plane)], [], velocity
    )
    first, second = pair_swap(first, second)
    factor, adj_down, left, rims, base, patch_map = call(
        with_sizes(matrix_kernel),
        [shape_of(*field)] * 3
        + [shape_of(5, rows, span), shape_of(*field), jax.ShapeDtypeStruct(plane, jnp.int32)],
        [],
        shape_coef,
        cotangent,
        velocity,
        patch_map,
    )
    down, mine, give = call(
        velocity_kernel,
        [shape_of(*field)] + [shape_of(7, rows, span // 2)] * 2,
        [],
        base,
        second,
        first,
        factor,
        rims,
    )
    mine, give = line_ends(mine, give)
    got = swap(give, 1)
    owned = broken.shape[0]
    devices = groups_x * groups_y
    patch_count = owned * devices
    half = (planes, rows, span // 2)
    adj_mine, new_mine, sums = call(
        with_sizes(functools.partial(own_half_kernel, patch_count)),
        [shape_of(*half), shape_of(*half), shape_of(PATCH_ROWS, patch_count // PATCH_ROWS)],
        [],
        factor,
        left,
        adj_down,
        down,
        mine,
        patch_map,
    )
    adj_got, new_got, sums = call(
        with_sizes(functools.partial(shares_kernel, patch_count)),
        [shape_of(*half), shape_of(*half), shape_of(devices, patch_count // PATCH_ROWS)],
        [],
        factor,
        left,
        adj_down,
        down,
        got,
        patch_map,
        sums,
    )
    first, second = call(
        adjoint_edges_kernel, [shape_of(*plane), shape_of(*plane)], [], adj_mine, adj_got
    )
    first, second = pair_swap(first, second)
    shares = lax.all_to_all(sums, ("gy", "gx"), 0, 0, tiled=True)
    norm_factor = 1.0 / math.sqrt(planes * groups_x * total_rows * span / (owned * devices))
    grad_velocity, new_velocity, weight = call(
        functools.partial(gradient_kernel, norm_factor),
        [shape_of(*field), shape_of(*field), shape_of(1, owned)],
        [],
        adj_mine,
        adj_got,
        new_mine,
        new_got,
        second,
        first,
        broken.reshape(1, owned),
    )
    (patch_sens,) = call(patch_kernel, [shape_of(1, owned)], [], shares, weight)
    return (new_velocity, grad_velocity, patch_sens.reshape(owned))


def solution(mesh):
    return jax.shard_map(
        local,
        mesh=mesh,
        in_specs=(
            P("gx", "gy", None),
            P("gx", "gy", None),
            P("gx", None),
            P("gx", None),
            P(("gx", "gy")),
        ),
        out_specs=(P("gx", "gy", None), P("gx", "gy", None), P(("gx", "gy"))),
        check_vma=False,
    )
```

```python
import functools
import math

import jax
import jax.numpy as jnp
from jax import lax
from jax.experimental import pallas as pl
from jax.experimental.pallas import tpu as pltpu
from jax.sharding import PartitionSpec as P

wall_coef = 0.2
span_coef = 0.15
wall_decay = 8.0
VMEM = pl.BlockSpec(memory_space=pltpu.VMEM)
F32 = jnp.float32
LANES = 128
PATCH_ROWS = 16


def shape_of(*dims):
    return jax.ShapeDtypeStruct(dims, F32)


def explicit(field, below, above):
    rows, span = field.shape
    row_ids = lax.broadcasted_iota(jnp.int32, (rows, span), 0)
    lower = jnp.where(row_ids == 0, below, pltpu.roll(field, 1, 0))
    upper = jnp.where(row_ids == rows - 1, above, pltpu.roll(field, rows - 1, 0))
    wall_term = upper + lower - 2.0 * field
    span_term = pltpu.roll(field, 1, 1) + pltpu.roll(field, span - 1, 1) - 2.0 * field
    return field + wall_coef * wall_term + span_coef * span_term


def edges(refs, k, field):
    first_ref, second_ref = refs
    rows = field.shape[0]
    even = lax.axis_index("gy") % 2 == 0
    low, high = field[:1], field[rows - 1 :]
    first_ref[k : k + 1, :] = jnp.where(even, high, low)
    second_ref[k : k + 1, :] = jnp.where(even, low, high)


def halo(first_ref, second_ref, k):
    position = lax.axis_index("gy")
    even = position % 2 == 0
    inner = (position > 0) & (position < lax.axis_size("gy") - 1)
    first = first_ref[k : k + 1, :]
    second = jnp.where(inner, second_ref[k : k + 1, :], 0.0)
    return jnp.where(even, second, first), jnp.where(even, first, second)


def near_swap(edge):
    return lax.ppermute(edge, "gy", [(i, i ^ 1) for i in range(lax.axis_size("gy"))])


def far_swap(edge):
    count_x, count = lax.axis_size("gx"), lax.axis_size("gy")
    pairs = []
    for i in range(count_x):
        for j in range(count):
            target = j + 1 if j % 2 else j - 1
            inside = 0 <= target < count
            pairs.append((i * count + j, i * count + target if inside else (i ^ 1) * count + j))
    return lax.ppermute(edge, ("gx", "gy"), pairs)


def pair_swap(first, second):
    return near_swap(first), far_swap(second)


def edge_kernel(velocity_ref, held_ref, first_ref, second_ref):
    for k in range(velocity_ref.shape[0]):
        held_ref[k] = velocity_ref[k]
        edges((first_ref, second_ref), k, velocity_ref[k])


def damping_rows(rows, total_rows):
    first = lax.axis_index("gy") * rows
    heights = (first + lax.broadcasted_iota(jnp.int32, (rows, 1), 0)).astype(F32)
    return jnp.exp(-wall_decay * heights / total_rows)


def matrix_kernel(
    stiffness, total_rows, coef_ref, target_ref, velocity_ref, map_ref,
    factor_ref, adj_down_ref, left_ref, rims_ref, base_ref, map_out_ref,
):
    map_out_ref[...] = map_ref[...]
    for k in range(velocity_ref.shape[0]):
        base_ref[k] = explicit(velocity_ref[k], 0.0, 0.0)
    planes, rows, span = target_ref.shape
    damping = damping_rows(rows, total_rows)
    factor = jnp.zeros((rows, span), F32)
    reduced = jnp.zeros((rows, span), F32)
    left = jnp.ones((rows, span), F32)
    for k in range(planes):
        diagonal = 1.0 + 2.0 * stiffness + coef_ref[k : k + 1, :] * damping
        factor = stiffness / (diagonal - stiffness * factor)
        reduced = (target_ref[k] + reduced) * factor
        left = left * factor
        factor_ref[k] = factor
        adj_down_ref[k] = reduced
        left_ref[k] = left
    value, right = reduced, factor
    rims_ref[1] = left
    rims_ref[2] = factor
    rims_ref[4] = reduced
    for k in range(planes - 2, -1, -1):
        factor = factor_ref[k]
        value = adj_down_ref[k] + factor * value
        left = left_ref[k] + factor * left
    rims_ref[0] = left
    rims_ref[3] = value


def velocity_kernel(base_ref, second_ref, first_ref, factor_ref, rims_ref, down_ref, mine_ref, give_ref):
    planes, rows, span = base_ref.shape
    row_ids = lax.broadcasted_iota(jnp.int32, (rows, span), 0)
    reduced = jnp.zeros((rows, span), F32)
    for k in range(planes):
        below, above = halo(first_ref, second_ref, k)
        outside = jnp.where(row_ids == 0, below, jnp.where(row_ids == rows - 1, above, 0.0))
        forcing = base_ref[k] + wall_coef * outside
        reduced = (forcing + reduced) * factor_ref[k]
        down_ref[k] = reduced
    value = reduced
    for k in range(planes - 2, -1, -1):
        value = down_ref[k] + factor_ref[k] * value
    pieces = [rims_ref[i] for i in range(5)] + [value, reduced]
    split(half_first(), pieces, mine_ref, give_ref)


def place():
    position = lax.axis_index("gx")
    return position % 2, position // 2


def split(first, pieces, mine_ref, give_ref):
    width = mine_ref.shape[2]
    for i, piece in enumerate(pieces):
        low, high = piece[:, :width], piece[:, width:]
        mine_ref[i] = jnp.where(first, low, high)
        give_ref[i] = jnp.where(first, high, low)


def joined(first, mine, other):
    return jnp.concatenate([jnp.where(first, mine, other), jnp.where(first, other, mine)], axis=1)


def merged(is_left, mine_ref, other_ref, tie_ref):
    left, right = [], []
    for i in range(7):
        mine, other = mine_ref[i], other_ref[i]
        left.append(jnp.where(is_left, mine, other))
        right.append(jnp.where(is_left, other, mine))
    top_l, cross_l, low_l, *sides_l = left
    top_r, cross_r, low_r, *sides_r = right
    inverse = 1.0 / (1.0 - low_l * top_r)
    to_left, to_right = cross_l * inverse, cross_r * inverse
    through_top, through_low = top_r * to_left, low_l * to_right
    tie_ref[0], tie_ref[1], tie_ref[2], tie_ref[3] = to_left, through_low, through_top, to_right
    block = [top_l + cross_l * through_top, cross_l * to_right, low_r + cross_r * through_low]
    for side in range(2):
        tops_l, lows_l = sides_l[2 * side], sides_l[2 * side + 1]
        tops_r, lows_r = sides_r[2 * side], sides_r[2 * side + 1]
        low = (lows_l + low_l * tops_r) * inverse
        top = (tops_r + top_r * lows_l) * inverse
        tie_ref[4 + 2 * side], tie_ref[5 + 2 * side] = low, top
        block += [tops_l + cross_l * top, lows_r + cross_r * low]
    return block


def untied(tie_ref, outer):
    inner = []
    for side in range(2):
        below, above = outer[2 * side], outer[2 * side + 1]
        low = tie_ref[4 + 2 * side] + tie_ref[0] * below + tie_ref[1] * above
        top = tie_ref[5 + 2 * side] + tie_ref[2] * below + tie_ref[3] * above
        inner.append((low, top))
    (low_a, top_a), (low_v, top_v) = inner
    return (
        [outer[0], top_a, outer[2], top_v],
        [low_a, outer[1], low_v, outer[3]],
    )


def chosen(is_left, pair):
    return [jnp.where(is_left, x, y) for x, y in zip(*pair)]


def half_first():
    core, chip = place()
    return (core + chip) % 2 == 0


def quarter_first():
    _, chip = place()
    return (chip + chip // 2) % 2 == 0


def core_kernel(mine_ref, got_ref, tie_ref, keep_ref, give_ref):
    core, _ = place()
    split(quarter_first(), merged(core == 0, mine_ref, got_ref, tie_ref), keep_ref, give_ref)


def chip_kernel(mine_ref, got_ref, tie_ref, block_ref):
    _, chip = place()
    for i, value in enumerate(merged(chip % 2 == 0, mine_ref, got_ref, tie_ref)):
        block_ref[i] = value


def four_kernel(mine_ref, got_ref, tie_ref, rim_ref):
    _, chip = place()
    top, _, low, *sides = merged(chip // 2 % 2 == 0, mine_ref, got_ref, tie_ref)
    is_left = chip < 4
    rim_ref[0] = jnp.where(is_left, low, top)
    rim_ref[1] = jnp.where(is_left, sides[1], sides[0])
    rim_ref[2] = jnp.where(is_left, sides[3], sides[2])


def middle_kernel(rim_ref, got_ref, four_tie_ref, chip_tie_ref, mine_ref, give_ref):
    _, chip = place()
    is_left = chip < 4
    rim, got = rim_ref[0], got_ref[0]
    inverse = 1.0 / (1.0 - rim * got)
    outer = []
    for side in (1, 2):
        across = (got_ref[side] + got * rim_ref[side]) * inverse
        outer += [jnp.where(is_left, 0.0, across), jnp.where(is_left, across, 0.0)]
    outer = chosen(chip // 2 % 2 == 0, untied(four_tie_ref, outer))
    left, right = untied(chip_tie_ref, outer)
    for i in range(4):
        mine_ref[i] = jnp.where(chip % 2 == 0, left[i], right[i])
        give_ref[i] = jnp.where(chip % 2 == 0, right[i], left[i])


def spread_kernel(low_part_ref, low_got_ref, high_part_ref, high_got_ref, tie_ref, mine_ref, give_ref):
    core, chip = place()
    first = quarter_first()
    is_low = chip < 4
    outer = [
        joined(
            first,
            jnp.where(is_low, low_part_ref[i], high_part_ref[i]),
            jnp.where(is_low, low_got_ref[i], high_got_ref[i]),
        )
        for i in range(4)
    ]
    left, right = untied(tie_ref, outer)
    for i in range(4):
        mine_ref[i] = jnp.where(core == 0, left[i], right[i])
        give_ref[i] = jnp.where(core == 0, right[i], left[i])


def swap(array, distance, high_distance=None):
    count = lax.axis_size("gx")
    high_distance = high_distance or distance
    pairs = [(i, i ^ (distance if i < count // 2 else high_distance)) for i in range(count)]
    return lax.ppermute(array, "gx", pairs)


def line_ends(mine, give):
    rows, width = mine.shape[1:]
    half = width // 2
    got = swap(give, 1)
    core_tie, part, give = call(
        core_kernel,
        [shape_of(8, rows, width), shape_of(7, rows, half), shape_of(7, rows, half)],
        [],
        mine,
        got,
    )
    got = swap(give, 3)
    chip_tie, block = call(
        chip_kernel, [shape_of(8, rows, half), shape_of(7, rows, half)], [], part, got
    )
    four = [shape_of(8, rows, half), shape_of(3, rows, half)]
    ends = [shape_of(4, rows, half)] * 2
    low_tie, low_rim = call(four_kernel, four, [], block, swap(block, 7, 1))
    from_low = swap(low_rim, 15)
    high_tie, high_rim = call(four_kernel, four, [], block, swap(block, 1, 7))
    from_high = swap(high_rim, 15)
    high_part, give = call(middle_kernel, ends, [], high_rim, from_low, high_tie, chip_tie)
    high_got = swap(give, 1, 3)
    low_part, give = call(middle_kernel, ends, [], low_rim, from_high, low_tie, chip_tie)
    low_got = swap(give, 3, 1)
    sides = (low_part, low_got, high_part, high_got)
    return call(spread_kernel, [shape_of(4, rows, width)] * 2, [], *sides, core_tie)


def lanes_of(is_mine, width):
    first = half_first() if is_mine else jnp.logical_not(half_first())
    return pl.ds(pl.multiple_of(jnp.where(first, 0, width), LANES), width)


def back_sweep(lanes, factor_ref, left_ref, down_ref, below, above, scale, out_ref):
    value = above
    for k in range(out_ref.shape[0] - 1, -1, -1):
        value = down_ref[k, :, lanes] + left_ref[k, :, lanes] * below + factor_ref[k, :, lanes] * value
        out_ref[k] = value * scale


def patch_sums(patch_count, total_rows, lanes, map_ref, adj_ref, new_ref, places_ref=None):
    planes, rows, width = adj_ref.shape
    damping = damping_rows(rows, total_rows)
    patch_rows = PATCH_ROWS
    patch_lanes = patch_count // patch_rows
    row_ids = lax.broadcasted_iota(jnp.int32, (patch_rows, width), 0)
    lane_ids = lax.broadcasted_iota(jnp.int32, (patch_lanes, width), 0)
    total = jnp.zeros((3 * patch_rows, patch_lanes), F32)
    for k in range(planes):
        cells = jnp.sum(adj_ref[k] * new_ref[k] * damping, axis=0, keepdims=True)
        patches = map_ref[k : k + 1, lanes]
        first = cells.astype(jnp.bfloat16).astype(F32)
        rest = cells - first
        second = rest.astype(jnp.bfloat16).astype(F32)
        third = rest - second
        in_row = row_ids == patches // patch_lanes
        parts = jnp.concatenate(
            [jnp.where(in_row, part, 0.0) for part in (first, second, third)], axis=0
        ).astype(jnp.bfloat16)
        if places_ref is None:
            places = jnp.where(lane_ids == patches % patch_lanes, 1.0, 0.0).astype(jnp.bfloat16)
        else:
            places = places_ref[k]
        total = total + lax.dot_general(
            parts, places, (((1,), (1,)), ((), ())), preferred_element_type=F32
        )
    return total[:patch_rows] + total[patch_rows : 2 * patch_rows] + total[2 * patch_rows :]


def own_half_kernel(
    patch_count, stiffness, total_rows, factor_ref, left_ref, adj_down_ref, down_ref, ends_ref, map_ref,
    adj_ref, new_ref, sums_ref, places_ref,
):
    lanes = lanes_of(True, adj_ref.shape[2])
    sweep = (lanes, factor_ref, left_ref)
    back_sweep(*sweep, adj_down_ref, ends_ref[0], ends_ref[1], 1.0 / stiffness, adj_ref)
    back_sweep(*sweep, down_ref, ends_ref[2], ends_ref[3], 1.0 / stiffness, new_ref)
    sums_ref[...] = patch_sums(patch_count, total_rows, lanes, map_ref, adj_ref, new_ref)
    other = lanes_of(False, adj_ref.shape[2])
    patch_lanes, width = places_ref.shape[1:]
    lane_ids = lax.broadcasted_iota(jnp.int32, (patch_lanes, width), 0)
    for k in range(places_ref.shape[0]):
        owners = lane_ids == map_ref[k : k + 1, other] % patch_lanes
        places_ref[k] = jnp.where(owners, 1.0, 0.0).astype(jnp.bfloat16)


def adjoint_edges_kernel(mine_ref, got_ref, first_ref, second_ref):
    for k in range(mine_ref.shape[0]):
        edges((first_ref, second_ref), k, joined(half_first(), mine_ref[k], got_ref[k]))


def shares_kernel(
    patch_count, stiffness, total_rows, factor_ref, left_ref, adj_down_ref, down_ref, ends_ref, map_ref, mine_ref, places_ref,
    adj_ref, new_ref, shares_ref,
):
    lanes = lanes_of(False, adj_ref.shape[2])
    sweep = (lanes, factor_ref, left_ref)
    back_sweep(*sweep, adj_down_ref, ends_ref[0], ends_ref[1], 1.0 / stiffness, adj_ref)
    back_sweep(*sweep, down_ref, ends_ref[2], ends_ref[3], 1.0 / stiffness, new_ref)
    sums = mine_ref[...] + patch_sums(
        patch_count, total_rows, lanes, map_ref, adj_ref, new_ref, places_ref
    )
    rows_here = sums.shape[0]
    for i in range(shares_ref.shape[0] // rows_here):
        shares_ref[i * rows_here : (i + 1) * rows_here, :] = sums


def gradient_kernel(
    norm_factor, adj_ref, adj_got_ref, new_in_ref, new_got_ref, second_ref, first_ref, broken_ref,
    out_ref, new_ref, weight_ref,
):
    for k in range(adj_ref.shape[0]):
        adjoint = joined(half_first(), adj_ref[k], adj_got_ref[k])
        out_ref[k] = explicit(adjoint, *halo(first_ref, second_ref, k))
        new_ref[k] = joined(half_first(), new_in_ref[k], new_got_ref[k])
    weight_ref[...] = -(1 - broken_ref[...]).astype(F32) * norm_factor


def patch_kernel(shares_ref, weight_ref, out_ref):
    owned = weight_ref.shape[1]
    width = shares_ref.shape[1]
    total = jnp.sum(shares_ref[...], axis=0, keepdims=True)
    total = jnp.broadcast_to(jnp.concatenate([total] * (LANES // width), axis=1), (8, LANES))
    shift = lax.rem(LANES - owned * lax.axis_index("gy"), LANES)
    out_ref[...] = weight_ref[...] * pltpu.roll(total, shift, 1)[:1, :owned]


def call(kernel, outs, scratch, *operands):
    return pl.pallas_call(
        kernel,
        out_shape=outs,
        in_specs=[VMEM] * len(operands),
        out_specs=[VMEM] * len(outs),
        scratch_shapes=scratch,
        compiler_params=pltpu.CompilerParams(vmem_limit_bytes=32 * 1024 * 1024),
    )(*operands)


def local(velocity, cotangent, shape_coef, patch_map, broken):
    planes, rows, span = velocity.shape
    groups_x = lax.axis_size("gx")
    groups_y = lax.axis_size("gy")
    total_rows = rows * groups_y
    stiffness = 3.0 * planes * planes
    field = (planes, rows, span)
    plane = (planes, span)

    def with_sizes(kernel):
        return lambda *refs: kernel(stiffness, total_rows, *refs)

    velocity, first, second = call(
        edge_kernel, [shape_of(*field), shape_of(*plane), shape_of(*plane)], [], velocity
    )
    first, second = pair_swap(first, second)
    factor, adj_down, left, rims, base, patch_map = call(
        with_sizes(matrix_kernel),
        [shape_of(*field)] * 3
        + [shape_of(5, rows, span), shape_of(*field), jax.ShapeDtypeStruct(plane, jnp.int32)],
        [],
        shape_coef,
        cotangent,
        velocity,
        patch_map,
    )
    down, mine, give = call(
        velocity_kernel,
        [shape_of(*field)] + [shape_of(7, rows, span // 2)] * 2,
        [],
        base,
        second,
        first,
        factor,
        rims,
    )
    mine, give = line_ends(mine, give)
    got = swap(give, 1)
    owned = broken.shape[0]
    devices = groups_x * groups_y
    patch_count = owned * devices
    half = (planes, rows, span // 2)
    adj_mine, new_mine, sums, places = call(
        with_sizes(functools.partial(own_half_kernel, patch_count)),
        [
            shape_of(*half),
            shape_of(*half),
            shape_of(PATCH_ROWS, patch_count // PATCH_ROWS),
            jax.ShapeDtypeStruct((planes, patch_count // PATCH_ROWS, span // 2), jnp.bfloat16),
        ],
        [],
        factor,
        left,
        adj_down,
        down,
        mine,
        patch_map,
    )
    adj_got, new_got, sums = call(
        with_sizes(functools.partial(shares_kernel, patch_count)),
        [shape_of(*half), shape_of(*half), shape_of(devices, patch_count // PATCH_ROWS)],
        [],
        factor,
        left,
        adj_down,
        down,
        got,
        patch_map,
        sums,
        places,
    )
    first, second = call(
        adjoint_edges_kernel, [shape_of(*plane), shape_of(*plane)], [], adj_mine, adj_got
    )
    first, second = pair_swap(first, second)
    shares = lax.all_to_all(sums, ("gy", "gx"), 0, 0, tiled=True)
    norm_factor = 1.0 / math.sqrt(planes * groups_x * total_rows * span / (owned * devices))
    grad_velocity, new_velocity, weight = call(
        functools.partial(gradient_kernel, norm_factor),
        [shape_of(*field), shape_of(*field), shape_of(1, owned)],
        [],
        adj_mine,
        adj_got,
        new_mine,
        new_got,
        second,
        first,
        broken.reshape(1, owned),
    )
    (patch_sens,) = call(patch_kernel, [shape_of(1, owned)], [], shares, weight)
    return (new_velocity, grad_velocity, patch_sens.reshape(owned))


def solution(mesh):
    return jax.shard_map(
        local,
        mesh=mesh,
        in_specs=(
            P("gx", "gy", None),
            P("gx", "gy", None),
            P("gx", None),
            P("gx", None),
            P(("gx", "gy")),
        ),
        out_specs=(P("gx", "gy", None), P("gx", "gy", None), P(("gx", "gy"))),
        check_vma=False,
    )
```
